128 devices in a mesh: wide: 32 (over y, z, core), mp: 4 (over x).
Axes of the slice: x: 4, y: 4, z: 4, core: 2. Of those that a mesh axis runs over, the one named last changes fastest.
Arguments:
- queries: bfloat16 [32, 128, 8192], P('wide', None, 'mp'), may hold values from -6 to 6
- own_keys: bfloat16 [32, 128, 1024], P('wide', None, 'mp'), may hold values from -6 to 6
- own_values: bfloat16 [32, 128, 1024], P('wide', None, 'mp'), may hold values from -6 to 6
- cart_keys: bfloat16 [512, 128, 1024], P('wide', None, 'mp'), may hold values from -6 to 6
- cart_values: bfloat16 [512, 128, 1024], P('wide', None, 'mp'), may hold values from -6 to 6
- block_ids: int32 [32, 16], P('wide'), may hold values from 0 to 511, as said below
- block_home: int32 [512], replicated, may hold values from 0 to 511, as said below
- query_len: int32 [32], P('wide'), may hold values from 32 to 128, as said below
- grad_out: bfloat16 [32, 128, 8192], P('wide', None, 'mp'), may hold values from -6 to 6
Outputs:
- attn_out: bfloat16 [32, 128, 8192], P('wide', None, 'mp')
- grad_queries: bfloat16 [32, 128, 8192], P('wide', None, 'mp')
- key_update: float32 [512, 128, 1024], P('wide', None, 'mp')
- value_update: float32 [512, 128, 1024], P('wide', None, 'mp')
The draws below stay inside these ranges and needn't reach their ends.
Inputs may be any that keep to these rules, and one draw needn't show every extreme that they name: `block_ids`: the 16 ids of a request are distinct, and the 1 request of one index of wide read the same 16 ids, each in an order of its own; their storage rows lie on exactly 16 owner devices, exactly 1 on each, the owner of id b being block_home[b] // 16. `block_home`: each storage row appears once. `query_len`: some request uses all 128 slots.
All inputs are finite; a program needn't handle non-finite values.
Results may differ from the reference program's by a relative error of at most 0.011.
Values may be sent and summed in bfloat16 or wider, within the bound.
No kernel may reach another device: no remote copies, remote signals or barrier semaphores. Data moves between devices by JAX's collectives and lax.ppermute only.
A program may use at most 128 MiB of HBM per device.

```python
import math
import jax
import jax.numpy as jnp
from jax import lax

QH = 64
KVH = 8
HD = 128
BLK_TOK = 128
SEL = 16
QLEN = 128
BLK_DEV = 16
REQ_DEV = 1
CAP = 1
BLOCKS = 512
REQUESTS = 32
N_WIDE = 32


def common_blocks(key):
    base = jax.random.permutation(jax.random.fold_in(key, 11), BLOCKS).astype(jnp.int32)
    groups = SEL // CAP
    favour = jax.random.randint(jax.random.fold_in(key, 12), (N_WIDE,), 0, 4) * 65536
    score = jax.random.randint(jax.random.fold_in(key, 13), (N_WIDE, N_WIDE), 0, 65536) + favour[None, :]
    score = score * N_WIDE + jnp.arange(N_WIDE, dtype=jnp.int32)[None, :]
    owners = jnp.argsort(-score, axis=1)[:, :groups].astype(jnp.int32)
    private = jax.random.randint(jax.random.fold_in(key, 14), (N_WIDE, groups, BLK_DEV), 0, 1048576)
    private = private * BLK_DEV + jnp.arange(BLK_DEV, dtype=jnp.int32)
    popular = jax.random.randint(jax.random.fold_in(key, 16), (N_WIDE, BLK_DEV), 0, 1048576)
    popular = popular * BLK_DEV + jnp.arange(BLK_DEV, dtype=jnp.int32)[None, :]
    by_owner = jnp.take(popular, owners, axis=0)
    coin = jax.random.randint(jax.random.fold_in(key, 17), (N_WIDE, groups, 1), 0, 4)
    slot_score = jnp.where(coin > 0, by_owner, private)
    local_rows = jnp.argsort(slot_score, axis=-1)[..., :CAP].astype(jnp.int32)
    shared = (owners[..., None] * BLK_DEV + local_rows).reshape(N_WIDE, SEL)
    row_high = shared[0, 0]
    row_low = shared[0, 1]
    place_high = jnp.argmax(base == row_high).astype(jnp.int32)
    home = base.at[place_high].set(base[BLOCKS - 1]).at[BLOCKS - 1].set(row_high)
    place_low = jnp.argmax(home == row_low).astype(jnp.int32)
    home = home.at[place_low].set(home[0]).at[0].set(row_low).astype(jnp.int32)
    storage = jnp.repeat(shared, REQ_DEV, axis=0)
    shuffle = jax.random.randint(jax.random.fold_in(key, 15), (REQUESTS, SEL), 0, 1048576)
    shuffle = shuffle * SEL + jnp.arange(SEL, dtype=jnp.int32)[None, :]
    order = jnp.argsort(shuffle, axis=-1)
    storage = jnp.take_along_axis(storage, order, axis=1)
    inverse = jnp.argsort(home).astype(jnp.int32)
    return (home, inverse[storage].astype(jnp.int32))


def draw_block_ids(key, part):
    return common_blocks(key)[1]


def draw_block_home(key, part):
    return common_blocks(key)[0]


def draw_query_len(key, part):
    key = jax.random.fold_in(key, 3)
    lengths = jax.random.randint(jax.random.fold_in(key, 1), (REQUESTS,), QLEN // 4, QLEN + 1)
    chosen = jax.random.randint(jax.random.fold_in(key, 2), (), 0, REQUESTS)
    return lengths.at[chosen].set(QLEN).astype(jnp.int32)


def draw_queries(key, part):
    key = jax.random.fold_in(key, 5)
    shape = (REQUESTS, QLEN, QH * HD)
    field = jnp.clip(jax.random.normal(jax.random.fold_in(key, 1), shape, jnp.float32), -6.0, 6.0)
    return field.astype(jnp.bfloat16)


def draw_cart_keys(key, part):
    key = jax.random.fold_in(key, 7)
    shape = (BLOCKS, BLK_TOK, KVH * HD)
    field = jnp.clip(jax.random.normal(jax.random.fold_in(key, 1), shape, jnp.float32), -6.0, 6.0)
    return field.astype(jnp.bfloat16)


def draw_grad_out(key, part):
    key = jax.random.fold_in(key, 9)
    shape = (REQUESTS, QLEN, QH * HD)
    field = jnp.clip(jax.random.normal(jax.random.fold_in(key, 1), shape, jnp.float32), -6.0, 6.0)
    return field.astype(jnp.bfloat16)


def block_scale(rng, dims, split, smallest, high):
    factor_of = 1.0
    for axis_at, blocks in split:
        draws = jax.random.uniform(jax.random.fold_in(jax.random.fold_in(rng, 6), axis_at), (blocks,), jnp.float32, smallest / len(split), high / len(split))
        factor_of = factor_of * jnp.repeat(jnp.exp(draws), dims[axis_at] // blocks).reshape((-1,) + (1,) * (len(dims) - 1 - axis_at))
    return factor_of


def scatter_about(own_key, extent, spread, bound, split=(), held_as=jnp.bfloat16):
    gain = block_scale(own_key, extent, split, -0.22, 0.18) if split else 1.0
    values = jax.random.normal(own_key, extent, jnp.float32) * spread * gain
    return jnp.minimum(jnp.maximum(values, -bound), bound).astype(held_as)


def setup_inputs(seed: int = 0) -> dict:
    arg_keys = jax.random.split(jax.random.key(seed), 10)
    return {
        "queries": draw_queries(jax.random.fold_in(arg_keys[9], 71), 0),
        "own_keys": scatter_about(arg_keys[1], (REQUESTS, QLEN, KVH * HD), 1.0, 6.0, ((0, 32), (2, 4))),
        "own_values": scatter_about(arg_keys[2], (REQUESTS, QLEN, KVH * HD), 1.0, 6.0, ((0, 32), (2, 4))),
        "cart_keys": draw_cart_keys(jax.random.fold_in(arg_keys[9], 71), 0),
        "cart_values": scatter_about(arg_keys[4], (BLOCKS, BLK_TOK, KVH * HD), 1.0, 6.0, ((0, 32), (2, 4))),
        "block_ids": draw_block_ids(jax.random.fold_in(arg_keys[9], 71), 0),
        "block_home": draw_block_home(jax.random.fold_in(arg_keys[9], 71), 0),
        "query_len": draw_query_len(jax.random.fold_in(arg_keys[9], 71), 0),
        "grad_out": draw_grad_out(jax.random.fold_in(arg_keys[9], 71), 0),
    }


def attend_head(query_rows, keys, values, key_seen, row_used, grad_rows, scale):
    length = query_rows.shape[0]
    head_size = keys.shape[1]
    repeat = query_rows.shape[1] // head_size
    query_flat = query_rows.reshape(length * repeat, head_size)
    grad_flat = grad_rows.reshape(length * repeat, head_size)
    seen_flat = jnp.repeat(key_seen, repeat, axis=0)
    used_flat = jnp.repeat(row_used, repeat, axis=0)
    scores = jnp.dot(query_flat, keys.T, preferred_element_type=jnp.float32) * scale
    scores = jnp.where(seen_flat, scores, -1e+30)
    top = lax.optimization_barrier(jnp.max(scores, axis=-1, keepdims=True))
    expo = jnp.exp(scores - top)
    prob = expo / lax.optimization_barrier(jnp.sum(expo, axis=-1, keepdims=True))
    prob_low = prob.astype(jnp.bfloat16)
    output = jnp.dot(prob_low, values, preferred_element_type=jnp.float32)
    output = jnp.where(used_flat[:, None], output, 0.0)
    masked = jnp.where(used_flat[:, None], grad_flat, jnp.zeros_like(grad_flat))
    dprob = jnp.dot(masked, values.T, preferred_element_type=jnp.float32)
    grad_value = jnp.dot(prob_low.T, masked, preferred_element_type=jnp.float32)
    delta = lax.optimization_barrier(jnp.sum(dprob * prob, axis=-1, keepdims=True))
    dscore = (prob * (dprob - delta)).astype(jnp.bfloat16)
    grad_query = jnp.dot(dscore, keys, preferred_element_type=jnp.float32) * scale
    grad_key = jnp.dot(dscore.T, query_flat, preferred_element_type=jnp.float32) * scale
    return (output.reshape(length, repeat * head_size), grad_query.reshape(length, repeat * head_size), grad_key, grad_value)

def attend_request(query_rows, own_k, own_v, cart_k, cart_v, used_len, grad_rows, head_size):
    length = query_rows.shape[0]
    cart_rows = cart_k.shape[0]
    groups = cart_k.shape[1] // head_size
    repeat = query_rows.shape[1] // cart_k.shape[1]
    scale = 1.0 / math.sqrt(head_size)
    positions = jnp.arange(length, dtype=jnp.int32)
    causal = (positions[None, :] <= positions[:, None]) & (positions[None, :] < used_len)
    key_seen = jnp.concatenate([jnp.ones((length, cart_rows), dtype=bool), causal], axis=1)
    row_used = positions < used_len
    outputs, grad_qs, grad_ks, grad_vs = ([], [], [], [])
    for group in range(groups):
        qcol = slice(group * repeat * head_size, (group + 1) * repeat * head_size)
        kcol = slice(group * head_size, (group + 1) * head_size)
        keys = jnp.concatenate([cart_k[:, kcol], own_k[:, kcol]], axis=0)
        values = jnp.concatenate([cart_v[:, kcol], own_v[:, kcol]], axis=0)
        output, grad_query, grad_key, grad_value = attend_head(query_rows[:, qcol], keys, values, key_seen, row_used, grad_rows[:, qcol], scale)
        outputs.append(output)
        grad_qs.append(grad_query)
        grad_ks.append(grad_key[:cart_rows])
        grad_vs.append(grad_value[:cart_rows])
    return (jnp.concatenate(outputs, axis=1), jnp.concatenate(grad_qs, axis=1), jnp.concatenate(grad_ks, axis=1), jnp.concatenate(grad_vs, axis=1))

def reference(queries, own_keys, own_values, cart_keys, cart_values, block_ids, block_home, query_len, grad_out):
    width = cart_keys.shape[2]
    block_tok = cart_keys.shape[1]

    def one_request(carry, inputs):
        query_rows, own_k, own_v, ids, used_len, grad_rows = inputs
        grad_k_all, grad_v_all = carry
        storage = block_home[ids].astype(jnp.int32)
        cart_k = cart_keys[storage].reshape(-1, width)
        cart_v = cart_values[storage].reshape(-1, width)
        output, grad_query, grad_key, grad_value = attend_request(query_rows, own_k, own_v, cart_k, cart_v, used_len, grad_rows, HD)
        grad_k_all = grad_k_all.at[storage].add(grad_key.reshape(-1, block_tok, width))
        grad_v_all = grad_v_all.at[storage].add(grad_value.reshape(-1, block_tok, width))
        return ((grad_k_all, grad_v_all), (output.astype(jnp.bfloat16), grad_query.astype(jnp.bfloat16)))
    start = (jnp.zeros(cart_keys.shape, jnp.float32), jnp.zeros(cart_keys.shape, jnp.float32))
    (grad_k_all, grad_v_all), (attn_out, grad_queries) = lax.scan(one_request, start, (queries, own_keys, own_values, block_ids, query_len, grad_out))
    count = 2.0 * grad_k_all.size
    total = jnp.sum(grad_k_all * grad_k_all) + jnp.sum(grad_v_all * grad_v_all)
    rms = jnp.sqrt(total / count + 1e-06)
    return (attn_out, grad_queries, grad_k_all / rms, grad_v_all / rms)
```

```python
import functools
import math

import jax
import jax.numpy as jnp
from jax import lax
from jax.experimental import pallas as pl
from jax.experimental.pallas import tpu as pltpu
from jax.sharding import PartitionSpec as P

HD = 128
SLICE = 16
HEADS = 2
KINDS = 2
MIB = 1024 * 1024


def nt(a, b):
    return lax.dot_general(a, b, (((1,), (1,)), ((), ())), preferred_element_type=jnp.float32)


def nn(a, b):
    return jnp.dot(a, b, preferred_element_type=jnp.float32)


def split_kernel(keys_ref, values_ref, tag_ref, out_ref, sems):
    blocks = keys_ref.shape[0]
    copies = []
    for m in range(out_ref.shape[0]):
        t, h, kind = m // 4, (m // 2) % 2, m % 2
        src = (keys_ref, values_ref)[kind]
        copies.append(
            pltpu.make_async_copy(
                src.at[:, pl.ds(t * SLICE, SLICE), pl.ds(h * HD, HD)],
                out_ref.at[m, pl.ds(0, blocks)],
                sems.at[2 * m],
            )
        )
        copies.append(
            pltpu.make_async_copy(tag_ref, out_ref.at[m, pl.ds(blocks, 1)], sems.at[2 * m + 1])
        )
    for copy in copies:
        copy.start()
    for copy in copies:
        copy.wait()


def split(cart_keys, cart_values, tag, count):
    blocks = cart_keys.shape[0]
    return pl.pallas_call(
        split_kernel,
        out_shape=jax.ShapeDtypeStruct((count, blocks + 1, SLICE, HD), jnp.bfloat16),
        in_specs=[pl.BlockSpec(memory_space=pl.ANY)] * 3,
        out_specs=pl.BlockSpec(memory_space=pl.ANY),
        scratch_shapes=[pltpu.SemaphoreType.DMA((2 * count,))],
        name="split_blocks",
    )(cart_keys, cart_values, tag)


def pick_kernel(index_ref, held_ref, out_ref):
    def step(n, carry):
        for u in range(8):
            out_ref[n * 8 + u] = held_ref[index_ref[n * 8 + u]]
        return carry

    lax.fori_loop(0, out_ref.shape[0] // 8, step, 0)


def pick(index, held):
    return pl.pallas_call(
        pick_kernel,
        out_shape=jax.ShapeDtypeStruct((index.shape[0],) + held.shape[1:], jnp.bfloat16),
        in_specs=[
            pl.BlockSpec(memory_space=pltpu.SMEM),
            pl.BlockSpec(memory_space=pltpu.VMEM),
        ],
        out_specs=pl.BlockSpec(memory_space=pltpu.VMEM),
        compiler_params=pltpu.CompilerParams(vmem_limit_bytes=16 * MIB),
        name="pick_requested",
    )(index, held)


def attend_kernel(
    length_ref,
    kv_ref,
    q_ref,
    qt_ref,
    gt_ref,
    own_k_ref,
    own_v_ref,
    out_ref,
    grad_q_ref,
    send_ref,
    score,
    expo,
    acc,
):
    used = length_ref[0]
    chunks = kv_ref.shape[0] // (HEADS * KINDS)
    chunk = kv_ref.shape[1]
    rows = q_ref.shape[1]
    queries = out_ref.shape[0]
    repeat = rows // queries
    own = own_k_ref.shape[0]
    scale = 1.0 / math.sqrt(HD)
    log2e = scale * math.log2(math.e)
    position = lax.rem(lax.broadcasted_iota(jnp.int32, (1, rows), 1), queries)
    row_used = position < used
    own_at = lax.broadcasted_iota(jnp.int32, (own, rows), 0)
    seen = (own_at <= position) & (own_at < used)
    for head in range(HEADS):
        lanes = slice(head * HD, (head + 1) * HD)
        own_k = own_k_ref[:, lanes]
        own_v = own_v_ref[:, lanes]
        qt = qt_ref[head]
        gt = gt_ref[head]
        at = lambda c, kind: (c * HEADS + head) * KINDS + kind
        own_s = jnp.where(seen, nn(own_k, qt), -1e30)
        top = jnp.max(own_s.reshape(own // 8, 8, rows), axis=0)
        for c in range(chunks):
            s = nn(kv_ref[at(c, 0)], qt)
            score[c] = s
            top = jnp.maximum(top, jnp.max(s.reshape(chunk // 8, 8, rows), axis=0))
        top = jnp.max(top, axis=0, keepdims=True) * log2e
        e = jnp.exp2(own_s * log2e - top)
        total = jnp.sum(e.reshape(own // 8, 8, rows), axis=0)
        own_e = e.astype(jnp.bfloat16)
        acc[...] = nn(own_v.T, own_e)
        for c in range(chunks):
            e = jnp.exp2(score[c] * log2e - top)
            total = total + jnp.sum(e.reshape(chunk // 8, 8, rows), axis=0)
            low = e.astype(jnp.bfloat16)
            expo[c] = low
            acc[...] += nn(kv_ref[at(c, 1)].T, low)
        inv = 1.0 / jnp.sum(total, axis=0, keepdims=True)
        gt32 = jnp.where(row_used, gt.astype(jnp.float32), 0.0)
        out = jnp.where(row_used, acc[...] * inv, 0.0)
        for r in range(repeat):
            cols = slice((head * repeat + r) * HD, (head * repeat + r + 1) * HD)
            out_ref[:, cols] = out[:, r * queries : (r + 1) * queries].T.astype(jnp.bfloat16)
        delta = jnp.sum(gt32 * out, axis=0, keepdims=True) * inv
        gs = (gt32 * inv).astype(jnp.bfloat16)
        ds = (own_e.astype(jnp.float32) * (nn(own_v, gs) - delta)).astype(jnp.bfloat16)
        acc[...] = nn(own_k.T, ds)
        for c in range(chunks):
            low = expo[c]
            send_ref[at(c, 1)] = nt(low, gs).astype(jnp.bfloat16)
            dp = nn(kv_ref[at(c, 1)], gs)
            ds = (low.astype(jnp.float32) * (dp - delta)).astype(jnp.bfloat16)
            send_ref[at(c, 0)] = (nn(ds, q_ref[head]) * scale).astype(jnp.bfloat16)
            acc[...] += nn(kv_ref[at(c, 0)].T, ds)
        grad = acc[...] * scale
        for r in range(repeat):
            cols = slice((head * repeat + r) * HD, (head * repeat + r + 1) * HD)
            grad_q_ref[:, cols] = grad[:, r * queries : (r + 1) * queries].T.astype(jnp.bfloat16)


def attend(length, kv, q, qt, gt, own_k, own_v, queries, width):
    count, chunk, _ = kv.shape
    rows = q.shape[1]
    chunks = count // (HEADS * KINDS)
    vmem = pl.BlockSpec(memory_space=pltpu.VMEM)
    return pl.pallas_call(
        attend_kernel,
        out_shape=(
            jax.ShapeDtypeStruct((queries, width), jnp.bfloat16),
            jax.ShapeDtypeStruct((queries, width), jnp.bfloat16),
            jax.ShapeDtypeStruct(kv.shape, jnp.bfloat16),
        ),
        in_specs=[pl.BlockSpec(memory_space=pltpu.SMEM)] + [vmem] * 6,
        out_specs=(vmem, vmem, vmem),
        scratch_shapes=[
            pltpu.VMEM((chunks, chunk, rows), jnp.float32),
            pltpu.VMEM((chunks, chunk, rows), jnp.bfloat16),
            pltpu.VMEM((HD, rows), jnp.float32),
        ],
        compiler_params=pltpu.CompilerParams(vmem_limit_bytes=48 * MIB),
        cost_estimate=pl.CostEstimate(
            flops=12 * 2 * HD * rows * (chunks * chunk + queries),
            bytes_accessed=8 * MIB,
            transcendentals=HEADS * rows * chunks * chunk,
        ),
        name="attend_forward_backward",
    )(length, kv, q, qt, gt, own_k, own_v)


def add_kernel(index_ref, got_ref, out_ref, square_ref, table):
    table[...] = jnp.zeros_like(table)

    def step(n, carry):
        for u in range(4):
            at = index_ref[n * 4 + u]
            table[at] += got_ref[n * 4 + u].astype(jnp.float32)
        return carry

    lax.fori_loop(0, got_ref.shape[0] // 4, step, 0)

    def finish(n, squares):
        rows = table[pl.ds(n * 8, 8)]
        out_ref[pl.ds(n * 8, 8)] = rows.astype(jnp.bfloat16)
        return squares + jnp.sum((rows * rows).reshape(8 * SLICE // 8, 8, HD), axis=0)

    square_ref[...] = lax.fori_loop(
        0, table.shape[0] // 8, finish, jnp.zeros(square_ref.shape, jnp.float32)
    )


def add_up(index, got, blocks):
    vmem = pl.BlockSpec(memory_space=pltpu.VMEM)
    return pl.pallas_call(
        add_kernel,
        out_shape=(
            jax.ShapeDtypeStruct((blocks, SLICE, HD), jnp.bfloat16),
            jax.ShapeDtypeStruct((8, HD), jnp.float32),
        ),
        in_specs=[pl.BlockSpec(memory_space=pltpu.SMEM), vmem],
        out_specs=(vmem, vmem),
        scratch_shapes=[pltpu.VMEM((blocks, SLICE, HD), jnp.float32)],
        compiler_params=pltpu.CompilerParams(vmem_limit_bytes=24 * MIB),
        name="add_over_readers",
    )(index, got)


def finish_kernel(count, square_ref, got_ref, key_ref, value_ref):
    total = jnp.sum(square_ref[...], axis=(0, 1), keepdims=True)
    inv = 1.0 / jnp.sqrt(total / count + 1e-6)
    for m in range(got_ref.shape[0]):
        t, h, kind = m // 4, (m // 2) % 2, m % 2
        dst = (key_ref, value_ref)[kind]
        part = got_ref[m].astype(jnp.float32) * inv.reshape(1, 1, 1)
        dst[:, t * SLICE : (t + 1) * SLICE, h * HD : (h + 1) * HD] = part


def finish(squares, got, block_tok, width, count):
    slices, blocks, _, _ = got.shape
    step = 4
    shape = jax.ShapeDtypeStruct((blocks, block_tok, width), jnp.float32)
    spec = pl.BlockSpec((step, block_tok, width), lambda n: (n, 0, 0))
    return pl.pallas_call(
        functools.partial(finish_kernel, count),
        out_shape=(shape, shape),
        grid=(blocks // step,),
        in_specs=[
            pl.BlockSpec((8, HD), lambda n: (0, 0)),
            pl.BlockSpec((slices, step, SLICE, HD), lambda n: (0, n, 0, 0)),
        ],
        out_specs=(spec, spec),
        compiler_params=pltpu.CompilerParams(vmem_limit_bytes=24 * MIB),
        name="normalize_updates",
    )(squares, got)


def wide_pairs(dy, dz, dc):
    pairs = []
    for y in range(4):
        for z in range(4):
            for c in range(2):
                to = (((y + dy) % 4) * 4 + (z + dz) % 4) * 2 + (c ^ dc)
                pairs.append(((y * 4 + z) * 2 + c, to))
    return pairs


def total_over_mesh(a):
    a = a + lax.ppermute(a, "wide", wide_pairs(0, 0, 1))
    a = a + sum(lax.ppermute(a, "mp", [(i, (i + d) % 4) for i in range(4)]) for d in (1, 2, 3))
    a = a + sum(lax.ppermute(a, "wide", wide_pairs(0, d, 0)) for d in (1, 2, 3))
    a = a + sum(lax.ppermute(a, "wide", wide_pairs(d, 0, 0)) for d in (1, 2, 3))
    return a


def swap(a):
    return lax.all_to_all(a, "wide", split_axis=0, concat_axis=0, tiled=True)


def heads_first(a, rows):
    length = a.shape[0]
    return a.reshape(length, HEADS, rows // length, HD).transpose(1, 2, 0, 3).reshape(HEADS, rows, HD)


def local(
    queries,
    own_keys,
    own_values,
    cart_keys,
    cart_values,
    block_ids,
    block_home,
    query_len,
    grad_out,
):
    wide_count = lax.axis_size("wide")
    blk_dev, block_tok, width = cart_keys.shape
    selected = block_ids.shape[1]
    all_blocks = block_home.shape[0]
    length = queries.shape[1]
    rows = length * queries.shape[2] // width
    lookup = block_ids[0][:, None] == jnp.arange(all_blocks, dtype=jnp.int32)
    storage = jnp.sum(jnp.where(lookup, block_home[None, :], 0), axis=-1)
    tag = jnp.stack([storage // blk_dev, storage % blk_dev]).astype(jnp.bfloat16)
    tag = jnp.pad(tag, ((0, SLICE - 2), (0, HD - selected)))[None]
    held = swap(split(cart_keys, cart_values, tag, wide_count))
    asked = held[:, blk_dev, :2, :selected].astype(jnp.int32)
    owner, row = asked[:, 0].reshape(-1), asked[:, 1].reshape(-1)
    picked = pick(
        owner * (blk_dev + 1) + row, held.reshape(wide_count * (blk_dev + 1), SLICE, HD)
    )
    kv = swap(picked.reshape(wide_count, selected * SLICE, HD))
    q = heads_first(queries[0], rows)
    qt = q.transpose(0, 2, 1)
    gt = heads_first(grad_out[0], rows).transpose(0, 2, 1)
    attn_out, grad_queries, send = attend(
        query_len, kv, q, qt, gt, own_keys[0], own_values[0], length, queries.shape[2]
    )
    got = swap(send)
    sums, squares = add_up(
        owner * blk_dev + row, got.reshape(wide_count * selected, SLICE, HD), all_blocks
    )
    back = swap(sums.reshape(wide_count, blk_dev, SLICE, HD))
    squares = total_over_mesh(squares)
    count = 2.0 * all_blocks * block_tok * width * lax.axis_size("mp")
    key_update, value_update = finish(squares, back, block_tok, width, count)
    return (attn_out[None], grad_queries[None], key_update, value_update)


def solution(mesh):
    shared = P("wide", None, "mp")
    return jax.shard_map(
        local,
        mesh=mesh,
        in_specs=(shared, shared, shared, shared, shared, P("wide", None), P(), P("wide"), shared),
        out_specs=(shared, shared, shared, shared),
        check_vma=False,
    )
```

```python
import functools
import math

import jax
import jax.numpy as jnp
from jax import lax
from jax.experimental import pallas as pl
from jax.experimental.pallas import tpu as pltpu
from jax.sharding import PartitionSpec as P

HD = 128
SLICE = 16
HEADS = 2
KINDS = 2
MIB = 1024 * 1024


def nt(a, b):
    return lax.dot_general(a, b, (((1,), (1,)), ((), ())), preferred_element_type=jnp.float32)


def nn(a, b):
    return jnp.dot(a, b, preferred_element_type=jnp.float32)


def split_kernel(ids_ref, home_ref, keys_ref, values_ref, out_ref, inside, parts, in_sems, out_sems):
    blocks, tokens, width = keys_ref.shape
    groups = tokens // SLICE
    arrive = []
    for t in range(groups):
        for kind, src in enumerate((keys_ref, values_ref)):
            copy = pltpu.make_async_copy(
                src.at[:, pl.ds(t * SLICE, SLICE)], inside.at[t, kind], in_sems.at[t, kind]
            )
            copy.start()
            arrive.append(copy)
    line = lax.broadcasted_iota(jnp.int32, (SLICE, HD), 0)
    lane = lax.broadcasted_iota(jnp.int32, (SLICE, HD), 1)
    tag = jnp.zeros((SLICE, HD), jnp.int32)
    for k in range(ids_ref.shape[1]):
        storage = home_ref[ids_ref[0, k]]
        owner = lax.div(storage, blocks)
        tag = jnp.where((line == 0) & (lane == k), owner, tag)
        tag = jnp.where((line == 1) & (lane == k), storage - owner * blocks, tag)
    tag = tag.astype(jnp.float32).astype(jnp.bfloat16)
    leave = []
    for t in range(groups):
        for kind in range(KINDS):
            arrive[t * KINDS + kind].wait()
        for part in range(HEADS * KINDS):
            m = t * HEADS * KINDS + part
            h, kind = part // KINDS, part % KINDS
            parts[m, pl.ds(0, blocks)] = inside[t, kind, :, :, h * HD : (h + 1) * HD]
            parts[m, blocks] = tag
            copy = pltpu.make_async_copy(parts.at[m], out_ref.at[m], out_sems.at[m])
            copy.start()
            leave.append(copy)
    for copy in leave:
        copy.wait()


def split(block_ids, block_home, cart_keys, cart_values, count):
    blocks, tokens, width = cart_keys.shape
    groups = tokens // SLICE
    smem = pl.BlockSpec(memory_space=pltpu.SMEM)
    hbm = pl.BlockSpec(memory_space=pltpu.HBM)
    return pl.pallas_call(
        split_kernel,
        out_shape=jax.ShapeDtypeStruct((count, blocks + 1, SLICE, HD), jnp.bfloat16),
        in_specs=[smem, smem, hbm, hbm],
        out_specs=hbm,
        scratch_shapes=[
            pltpu.VMEM((groups, KINDS, blocks, SLICE, width), jnp.bfloat16),
            pltpu.VMEM((count, blocks + 1, SLICE, HD), jnp.bfloat16),
            pltpu.SemaphoreType.DMA((groups, KINDS)),
            pltpu.SemaphoreType.DMA((count,)),
        ],
        compiler_params=pltpu.CompilerParams(vmem_limit_bytes=16 * MIB),
        name="split_blocks",
    )(block_ids, block_home, cart_keys, cart_values)


def pick_kernel(index_ref, held_ref, out_ref, buffer, sems):
    parts = sems.shape[0]
    size = out_ref.shape[0] // parts
    copies = []
    for part in range(parts):

        def step(n, carry):
            for u in range(16):
                at = part * size + n * 16 + u
                buffer[at] = held_ref[index_ref[at]]
            return carry

        lax.fori_loop(0, size // 16, step, 0)
        at = pl.ds(part * size, size)
        copies.append(pltpu.make_async_copy(buffer.at[at], out_ref.at[at], sems.at[part]))
        copies[-1].start()
    for copy in copies:
        copy.wait()


def pick(index, held):
    shape = (index.shape[0],) + held.shape[1:]
    return pl.pallas_call(
        pick_kernel,
        out_shape=jax.ShapeDtypeStruct(shape, jnp.bfloat16),
        in_specs=[
            pl.BlockSpec(memory_space=pltpu.SMEM),
            pl.BlockSpec(memory_space=pltpu.VMEM),
        ],
        out_specs=pl.BlockSpec(memory_space=pltpu.HBM),
        scratch_shapes=[pltpu.VMEM(shape, jnp.bfloat16), pltpu.SemaphoreType.DMA((4,))],
        compiler_params=pltpu.CompilerParams(vmem_limit_bytes=16 * MIB),
        name="pick_requested",
    )(index, held)


def attend_kernel(
    length_ref,
    kv_ref,
    q_ref,
    qt_ref,
    gt_ref,
    own_k_ref,
    own_v_ref,
    out_ref,
    grad_q_ref,
    send_ref,
    score,
    expo,
    acc,
    gt_in,
    out_buf,
    grad_buf,
    send_buf,
    gt_sem,
    out_sems,
    send_sems,
):
    load_gt = pltpu.make_async_copy(gt_ref, gt_in, gt_sem)
    load_gt.start()
    copies = []

    def leave(src, dst, sem):
        copies.append(pltpu.make_async_copy(src, dst, sem))
        copies[-1].start()

    used = length_ref[0]
    chunks = kv_ref.shape[0] // (HEADS * KINDS)
    chunk = kv_ref.shape[1]
    rows = q_ref.shape[1]
    queries = out_ref.shape[0]
    repeat = rows // queries
    own = own_k_ref.shape[0]
    scale = 1.0 / math.sqrt(HD)
    log2e = scale * math.log2(math.e)
    position = lax.rem(lax.broadcasted_iota(jnp.int32, (1, rows), 1), queries)
    row_used = position < used
    own_at = lax.broadcasted_iota(jnp.int32, (own, rows), 0)
    seen = (own_at <= position) & (own_at < used)
    for head in range(HEADS):
        lanes = slice(head * HD, (head + 1) * HD)
        own_k = own_k_ref[:, lanes]
        own_v = own_v_ref[:, lanes]
        qt = qt_ref[head]
        at = lambda c, kind: (c * HEADS + head) * KINDS + kind
        own_s = jnp.where(seen, nn(own_k, qt), -1e30)
        top = jnp.max(own_s.reshape(own // 8, 8, rows), axis=0)
        for c in range(chunks):
            s = nn(kv_ref[at(c, 0)], qt)
            score[c] = s
            top = jnp.maximum(top, jnp.max(s.reshape(chunk // 8, 8, rows), axis=0))
        top = jnp.max(top, axis=0, keepdims=True) * log2e
        e = jnp.exp2(own_s * log2e - top)
        total = jnp.sum(e.reshape(own // 8, 8, rows), axis=0)
        own_e = e.astype(jnp.bfloat16)
        acc[...] = nn(own_v.T, own_e)
        for c in range(chunks):
            e = jnp.exp2(score[c] * log2e - top)
            total = total + jnp.sum(e.reshape(chunk // 8, 8, rows), axis=0)
            low = e.astype(jnp.bfloat16)
            expo[c] = low
            acc[...] += nn(kv_ref[at(c, 1)].T, low)
        inv = 1.0 / jnp.sum(total, axis=0, keepdims=True)
        if head == 0:
            load_gt.wait()
        gt32 = jnp.where(row_used, gt_in[head].astype(jnp.float32), 0.0)
        out = jnp.where(row_used, acc[...] * inv, 0.0)
        for r in range(repeat):
            cols = slice((head * repeat + r) * HD, (head * repeat + r + 1) * HD)
            out_buf[:, cols] = out[:, r * queries : (r + 1) * queries].T.astype(jnp.bfloat16)
        half = pl.ds(head * repeat * HD, repeat * HD)
        leave(out_buf.at[:, half], out_ref.at[:, half], out_sems.at[0, head])
        delta = jnp.sum(gt32 * out, axis=0, keepdims=True) * inv
        gs = (gt32 * inv).astype(jnp.bfloat16)
        ds = (own_e.astype(jnp.float32) * (nn(own_v, gs) - delta)).astype(jnp.bfloat16)
        acc[...] = nn(own_k.T, ds)
        for c in range(chunks):
            low = expo[c]
            send_buf[at(c, 1)] = nt(low, gs).astype(jnp.bfloat16)
            dp = nn(kv_ref[at(c, 1)], gs)
            ds = (low.astype(jnp.float32) * (dp - delta)).astype(jnp.bfloat16)
            send_buf[at(c, 0)] = (nn(ds, q_ref[head]) * scale).astype(jnp.bfloat16)
            pair = pl.ds(at(c, 0), KINDS)
            leave(send_buf.at[pair], send_ref.at[pair], send_sems.at[c * HEADS + head])
            acc[...] += nn(kv_ref[at(c, 0)].T, ds)
        grad = acc[...] * scale
        for r in range(repeat):
            cols = slice((head * repeat + r) * HD, (head * repeat + r + 1) * HD)
            grad_buf[:, cols] = grad[:, r * queries : (r + 1) * queries].T.astype(jnp.bfloat16)
        leave(grad_buf.at[:, half], grad_q_ref.at[:, half], out_sems.at[1, head])
    for copy in copies:
        copy.wait()


def attend(length, kv, q, qt, gt, own_k, own_v, queries, width):
    count, chunk, _ = kv.shape
    rows = q.shape[1]
    chunks = count // (HEADS * KINDS)
    vmem = pl.BlockSpec(memory_space=pltpu.VMEM)
    hbm = pl.BlockSpec(memory_space=pltpu.HBM)
    return pl.pallas_call(
        attend_kernel,
        out_shape=(
            jax.ShapeDtypeStruct((queries, width), jnp.bfloat16),
            jax.ShapeDtypeStruct((queries, width), jnp.bfloat16),
            jax.ShapeDtypeStruct(kv.shape, jnp.bfloat16),
        ),
        in_specs=[pl.BlockSpec(memory_space=pltpu.SMEM), vmem, vmem, vmem, hbm, vmem, vmem],
        out_specs=(hbm, hbm, hbm),
        scratch_shapes=[
            pltpu.VMEM((chunks, chunk, rows), jnp.float32),
            pltpu.VMEM((chunks, chunk, rows), jnp.bfloat16),
            pltpu.VMEM((HD, rows), jnp.float32),
            pltpu.VMEM(gt.shape, jnp.bfloat16),
            pltpu.VMEM((queries, width), jnp.bfloat16),
            pltpu.VMEM((queries, width), jnp.bfloat16),
            pltpu.VMEM(kv.shape, jnp.bfloat16),
            pltpu.SemaphoreType.DMA,
            pltpu.SemaphoreType.DMA((2, HEADS)),
            pltpu.SemaphoreType.DMA((chunks * HEADS,)),
        ],
        compiler_params=pltpu.CompilerParams(vmem_limit_bytes=48 * MIB),
        cost_estimate=pl.CostEstimate(
            flops=12 * 2 * HD * rows * (chunks * chunk + queries),
            bytes_accessed=8 * MIB,
            transcendentals=HEADS * rows * chunks * chunk,
        ),
        name="attend_forward_backward",
    )(length, kv, q, qt, gt, own_k, own_v)


def add_kernel(index_ref, got_ref, out_ref, square_ref, table, buffer, sems):
    selected = index_ref.shape[1]
    parts = sems.shape[0]
    size = out_ref.shape[0] // parts
    table[...] = jnp.zeros_like(table)

    def step(n, carry):
        at = [index_ref[n, k] for k in range(selected)]
        sums = [table[at[k]] + got_ref[n, k].astype(jnp.float32) for k in range(selected)]
        for k in range(selected):
            table[at[k]] = sums[k]
        return carry

    lax.fori_loop(0, got_ref.shape[0], step, 0)
    squares = jnp.zeros(square_ref.shape, jnp.float32)
    copies = []
    for part in range(parts):

        def finish(n, squares):
            at = pl.ds(part * size + n * 8, 8)
            rows = table[at]
            buffer[at] = rows.astype(jnp.bfloat16)
            return squares + jnp.sum((rows * rows).reshape(SLICE, 8, HD), axis=0)

        squares = lax.fori_loop(0, size // 8, finish, squares)
        at = pl.ds(part * size, size)
        copies.append(pltpu.make_async_copy(buffer.at[at], out_ref.at[at], sems.at[part]))
        copies[-1].start()
    square_ref[...] = squares
    for copy in copies:
        copy.wait()


def add_up(index, got, blocks):
    vmem = pl.BlockSpec(memory_space=pltpu.VMEM)
    return pl.pallas_call(
        add_kernel,
        out_shape=(
            jax.ShapeDtypeStruct((blocks, SLICE, HD), jnp.bfloat16),
            jax.ShapeDtypeStruct((8, HD), jnp.float32),
        ),
        in_specs=[pl.BlockSpec(memory_space=pltpu.SMEM), vmem],
        out_specs=(pl.BlockSpec(memory_space=pltpu.HBM), vmem),
        scratch_shapes=[
            pltpu.VMEM((blocks, SLICE, HD), jnp.float32),
            pltpu.VMEM((blocks, SLICE, HD), jnp.bfloat16),
            pltpu.SemaphoreType.DMA((4,)),
        ],
        compiler_params=pltpu.CompilerParams(vmem_limit_bytes=24 * MIB),
        name="add_over_readers",
    )(index, got)


def finish_kernel(count, square_ref, got_ref, key_ref, value_ref):
    total = jnp.sum(square_ref[...], axis=(0, 1), keepdims=True)
    inv = 1.0 / jnp.sqrt(total / count + 1e-6)
    for m in range(got_ref.shape[0]):
        t, h, kind = m // 4, (m // 2) % 2, m % 2
        dst = (key_ref, value_ref)[kind]
        part = got_ref[m].astype(jnp.float32) * inv.reshape(1, 1, 1)
        dst[:, t * SLICE : (t + 1) * SLICE, h * HD : (h + 1) * HD] = part


def finish(squares, got, block_tok, width, count):
    slices, blocks, _, _ = got.shape
    step = 4
    shape = jax.ShapeDtypeStruct((blocks, block_tok, width), jnp.float32)
    spec = pl.BlockSpec((step, block_tok, width), lambda n: (n, 0, 0))
    return pl.pallas_call(
        functools.partial(finish_kernel, count),
        out_shape=(shape, shape),
        grid=(blocks // step,),
        in_specs=[
            pl.BlockSpec((8, HD), lambda n: (0, 0)),
            pl.BlockSpec((slices, step, SLICE, HD), lambda n: (0, n, 0, 0)),
        ],
        out_specs=(spec, spec),
        compiler_params=pltpu.CompilerParams(vmem_limit_bytes=24 * MIB),
        name="normalize_updates",
    )(squares, got)


def wide_pairs(dy, dz, dc):
    pairs = []
    for y in range(4):
        for z in range(4):
            for c in range(2):
                to = (((y + dy) % 4) * 4 + (z + dz) % 4) * 2 + (c ^ dc)
                pairs.append(((y * 4 + z) * 2 + c, to))
    return pairs


def total_over_mesh(a):
    a = a + lax.ppermute(a, "wide", wide_pairs(0, 0, 1))
    a = a + sum(lax.ppermute(a, "mp", [(i, (i + d) % 4) for i in range(4)]) for d in (1, 2, 3))
    shifts = [(dy, dz) for dy in range(4) for dz in range(4) if (dy, dz) != (0, 0)]
    return a + sum(lax.ppermute(a, "wide", wide_pairs(dy, dz, 0)) for dy, dz in shifts)


def swap(a):
    return lax.all_to_all(a, "wide", split_axis=0, concat_axis=0, tiled=True)


def heads_first(a, rows):
    length = a.shape[0]
    return a.reshape(length, HEADS, rows // length, HD).transpose(1, 2, 0, 3).reshape(HEADS, rows, HD)


def local(
    queries,
    own_keys,
    own_values,
    cart_keys,
    cart_values,
    block_ids,
    block_home,
    query_len,
    grad_out,
):
    wide_count = lax.axis_size("wide")
    blk_dev, block_tok, width = cart_keys.shape
    selected = block_ids.shape[1]
    all_blocks = block_home.shape[0]
    length = queries.shape[1]
    rows = length * queries.shape[2] // width
    held = swap(split(block_ids, block_home, cart_keys, cart_values, wide_count))
    asked = held[:, blk_dev, :2, :selected].astype(jnp.int32)
    owner, row = asked[:, 0], asked[:, 1]
    picked = pick(
        (owner * (blk_dev + 1) + row).reshape(-1),
        held.reshape(wide_count * (blk_dev + 1), SLICE, HD),
    )
    kv = swap(picked.reshape(wide_count, selected * SLICE, HD))
    q = heads_first(queries[0], rows)
    qt = q.transpose(0, 2, 1)
    gt = heads_first(grad_out[0], rows).transpose(0, 2, 1)
    attn_out, grad_queries, send = attend(
        query_len, kv, q, qt, gt, own_keys[0], own_values[0], length, queries.shape[2]
    )
    got = swap(send)
    sums, squares = add_up(
        owner * blk_dev + row, got.reshape(wide_count, selected, SLICE, HD), all_blocks
    )
    back = swap(sums.reshape(wide_count, blk_dev, SLICE, HD))
    squares = total_over_mesh(squares)
    count = 2.0 * all_blocks * block_tok * width * lax.axis_size("mp")
    key_update, value_update = finish(squares, back, block_tok, width, count)
    return (attn_out[None], grad_queries[None], key_update, value_update)


def solution(mesh):
    shared = P("wide", None, "mp")
    return jax.shard_map(
        local,
        mesh=mesh,
        in_specs=(shared, shared, shared, shared, shared, P("wide", None), P(), P("wide"), shared),
        out_specs=(shared, shared, shared, shared),
        check_vma=False,
    )
```

```python
import functools
import math

import jax
import jax.numpy as jnp
from jax import lax
from jax.experimental import pallas as pl
from jax.experimental.pallas import tpu as pltpu
from jax.sharding import PartitionSpec as P

HD = 128
SLICE = 16
HEADS = 2
KINDS = 2
MIB = 1024 * 1024


def nt(a, b):
    return lax.dot_general(a, b, (((1,), (1,)), ((), ())), preferred_element_type=jnp.float32)


def nn(a, b):
    return jnp.dot(a, b, preferred_element_type=jnp.float32)


def split_kernel(ids_ref, home_ref, keys_ref, values_ref, out_ref, inside, parts, in_sems, out_sems):
    blocks, tokens, width = keys_ref.shape
    groups = tokens // SLICE
    arrive = []
    for t in range(groups):
        for kind, src in enumerate((keys_ref, values_ref)):
            copy = pltpu.make_async_copy(
                src.at[:, pl.ds(t * SLICE, SLICE)], inside.at[t, kind], in_sems.at[t, kind]
            )
            copy.start()
            arrive.append(copy)
    line = lax.broadcasted_iota(jnp.int32, (SLICE, HD), 0)
    lane = lax.broadcasted_iota(jnp.int32, (SLICE, HD), 1)
    tag = jnp.zeros((SLICE, HD), jnp.int32)
    for k in range(ids_ref.shape[1]):
        storage = home_ref[ids_ref[0, k]]
        owner = lax.div(storage, blocks)
        tag = jnp.where((line == 0) & (lane == k), owner, tag)
        tag = jnp.where((line == 1) & (lane == k), storage - owner * blocks, tag)
    tag = tag.astype(jnp.float32).astype(jnp.bfloat16)
    leave = []
    for t in range(groups):
        for kind in range(KINDS):
            arrive[t * KINDS + kind].wait()
        for part in range(HEADS * KINDS):
            m = t * HEADS * KINDS + part
            h, kind = part // KINDS, part % KINDS
            parts[m, pl.ds(0, blocks)] = inside[t, kind, :, :, h * HD : (h + 1) * HD]
            parts[m, blocks] = tag
            copy = pltpu.make_async_copy(parts.at[m], out_ref.at[m], out_sems.at[m])
            copy.start()
            leave.append(copy)
    for copy in leave:
        copy.wait()


def split(block_ids, block_home, cart_keys, cart_values, count):
    blocks, tokens, width = cart_keys.shape
    groups = tokens // SLICE
    smem = pl.BlockSpec(memory_space=pltpu.SMEM)
    hbm = pl.BlockSpec(memory_space=pltpu.HBM)
    return pl.pallas_call(
        split_kernel,
        out_shape=jax.ShapeDtypeStruct((count, blocks + 1, SLICE, HD), jnp.bfloat16),
        in_specs=[smem, smem, hbm, hbm],
        out_specs=hbm,
        scratch_shapes=[
            pltpu.VMEM((groups, KINDS, blocks, SLICE, width), jnp.bfloat16),
            pltpu.VMEM((count, blocks + 1, SLICE, HD), jnp.bfloat16),
            pltpu.SemaphoreType.DMA((groups, KINDS)),
            pltpu.SemaphoreType.DMA((count,)),
        ],
        name="split_blocks",
    )(block_ids, block_home, cart_keys, cart_values)


def pick_kernel(index_ref, held_ref, out_ref):
    def step(n, carry):
        for u in range(16):
            out_ref[n * 16 + u] = held_ref[index_ref[n * 16 + u]]
        return carry

    lax.fori_loop(0, out_ref.shape[0] // 16, step, 0)


def pick(index, held):
    vmem = pl.BlockSpec(memory_space=pltpu.VMEM)
    return pl.pallas_call(
        pick_kernel,
        out_shape=jax.ShapeDtypeStruct((index.shape[0],) + held.shape[1:], jnp.bfloat16),
        in_specs=[pl.BlockSpec(memory_space=pltpu.SMEM), vmem],
        out_specs=vmem,
        compiler_params=pltpu.CompilerParams(vmem_limit_bytes=16 * MIB),
        name="pick_requested",
    )(index, held)


def attend_kernel(
    length_ref,
    kv_ref,
    q_ref,
    g_ref,
    own_k_ref,
    own_v_ref,
    out_ref,
    grad_q_ref,
    send_ref,
    score,
    expo,
    acc,
    q_rows,
    g_cols,
):
    used = length_ref[0]
    chunks = kv_ref.shape[0] // (HEADS * KINDS)
    chunk = kv_ref.shape[1]
    rows = q_rows.shape[0]
    queries = q_ref.shape[0]
    repeat = rows // queries
    own = own_k_ref.shape[0]
    scale = 1.0 / math.sqrt(HD)
    log2e = scale * math.log2(math.e)
    position = lax.rem(lax.broadcasted_iota(jnp.int32, (1, rows), 1), queries)
    row_used = position < used
    own_at = lax.broadcasted_iota(jnp.int32, (own, rows), 0)
    seen = (own_at <= position) & (own_at < used)
    for head in range(HEADS):
        lanes = slice(head * HD, (head + 1) * HD)
        own_k = own_k_ref[:, lanes]
        own_v = own_v_ref[:, lanes]
        at = lambda c, kind: (c * HEADS + head) * KINDS + kind
        for r in range(repeat):
            cols = slice((head * repeat + r) * HD, (head * repeat + r + 1) * HD)
            q_rows[r * queries : (r + 1) * queries] = q_ref[:, cols]
            g_cols[:, r * queries : (r + 1) * queries] = g_ref[:, cols].T
        own_s = jnp.where(seen, nt(own_k, q_rows[...]), -1e30)
        top = jnp.max(own_s.reshape(own // 8, 8, rows), axis=0)
        for c in range(chunks):
            s = nt(kv_ref[at(c, 0)], q_rows[...])
            score[c] = s
            top = jnp.maximum(top, jnp.max(s.reshape(chunk // 8, 8, rows), axis=0))
        top = jnp.max(top, axis=0, keepdims=True) * log2e
        e = jnp.exp2(own_s * log2e - top)
        total = jnp.sum(e.reshape(own // 8, 8, rows), axis=0)
        own_e = e.astype(jnp.bfloat16)
        acc[...] = nn(own_v.T, own_e)
        for c in range(chunks):
            e = jnp.exp2(score[c] * log2e - top)
            total = total + jnp.sum(e.reshape(chunk // 8, 8, rows), axis=0)
            low = e.astype(jnp.bfloat16)
            expo[c] = low
            acc[...] += nn(kv_ref[at(c, 1)].T, low)
        inv = 1.0 / jnp.sum(total, axis=0, keepdims=True)
        g = jnp.where(row_used, g_cols[...].astype(jnp.float32), 0.0)
        out = jnp.where(row_used, acc[...] * inv, 0.0)
        for r in range(repeat):
            cols = slice((head * repeat + r) * HD, (head * repeat + r + 1) * HD)
            out_ref[:, cols] = out[:, r * queries : (r + 1) * queries].T.astype(jnp.bfloat16)
        delta = jnp.sum(g * out, axis=0, keepdims=True) * inv
        gs = (g * inv).astype(jnp.bfloat16)
        ds = (own_e.astype(jnp.float32) * (nn(own_v, gs) - delta)).astype(jnp.bfloat16)
        acc[...] = nn(own_k.T, ds)
        for c in range(chunks):
            low = expo[c]
            send_ref[at(c, 1)] = nt(low, gs).astype(jnp.bfloat16)
            dp = nn(kv_ref[at(c, 1)], gs)
            ds = (low.astype(jnp.float32) * (dp - delta)).astype(jnp.bfloat16)
            send_ref[at(c, 0)] = (nn(ds, q_rows[...]) * scale).astype(jnp.bfloat16)
            acc[...] += nn(kv_ref[at(c, 0)].T, ds)
        grad = acc[...] * scale
        for r in range(repeat):
            cols = slice((head * repeat + r) * HD, (head * repeat + r + 1) * HD)
            grad_q_ref[:, cols] = grad[:, r * queries : (r + 1) * queries].T.astype(jnp.bfloat16)


def attend(length, kv, q, g, own_k, own_v):
    count, chunk, _ = kv.shape
    queries, width = q.shape
    rows = queries * width // (HEADS * HD)
    chunks = count // (HEADS * KINDS)
    vmem = pl.BlockSpec(memory_space=pltpu.VMEM)
    return pl.pallas_call(
        attend_kernel,
        out_shape=(
            jax.ShapeDtypeStruct(q.shape, jnp.bfloat16),
            jax.ShapeDtypeStruct(q.shape, jnp.bfloat16),
            jax.ShapeDtypeStruct(kv.shape, jnp.bfloat16),
        ),
        in_specs=[pl.BlockSpec(memory_space=pltpu.SMEM)] + [vmem] * 5,
        out_specs=(vmem, vmem, vmem),
        scratch_shapes=[
            pltpu.VMEM((chunks, chunk, rows), jnp.float32),
            pltpu.VMEM((chunks, chunk, rows), jnp.bfloat16),
            pltpu.VMEM((HD, rows), jnp.float32),
            pltpu.VMEM((rows, HD), jnp.bfloat16),
            pltpu.VMEM((HD, rows), jnp.bfloat16),
        ],
        compiler_params=pltpu.CompilerParams(vmem_limit_bytes=48 * MIB),
        cost_estimate=pl.CostEstimate(
            flops=12 * 2 * HD * rows * (chunks * chunk + queries),
            bytes_accessed=8 * MIB,
            transcendentals=HEADS * rows * chunks * chunk,
        ),
        name="attend_forward_backward",
    )(length, kv, q, g, own_k, own_v)


def add_kernel(index_ref, got_ref, out_ref, table):
    selected = index_ref.shape[1]
    owners, blocks = out_ref.shape[0], out_ref.shape[1] - 1
    table[...] = jnp.zeros_like(table)

    def step(n, carry):
        at = [index_ref[n, k] for k in range(selected)]
        sums = [table[at[k]] + got_ref[n, k].astype(jnp.float32) for k in range(selected)]
        for k in range(selected):
            table[at[k]] = sums[k]
        return carry

    lax.fori_loop(0, got_ref.shape[0], step, 0)

    def finish(n, squares):
        rows = table[pl.ds(n * blocks, blocks)]
        out_ref[n, pl.ds(0, blocks)] = rows.astype(jnp.bfloat16)
        return squares + jnp.sum((rows * rows).reshape(blocks * SLICE // 8, 8, HD), axis=0)

    squares = lax.fori_loop(0, owners, finish, jnp.zeros((8, HD), jnp.float32))
    high = squares.astype(jnp.bfloat16).astype(jnp.float32)
    tag = jnp.concatenate([high, squares - high], axis=0).astype(jnp.bfloat16)
    for n in range(owners):
        out_ref[n, blocks] = tag


def add_up(index, got, blk_dev):
    count = got.shape[0]
    vmem = pl.BlockSpec(memory_space=pltpu.VMEM)
    return pl.pallas_call(
        add_kernel,
        out_shape=jax.ShapeDtypeStruct((count, blk_dev + 1, SLICE, HD), jnp.bfloat16),
        in_specs=[pl.BlockSpec(memory_space=pltpu.SMEM), vmem],
        out_specs=vmem,
        scratch_shapes=[pltpu.VMEM((count * blk_dev, SLICE, HD), jnp.float32)],
        compiler_params=pltpu.CompilerParams(vmem_limit_bytes=24 * MIB),
        name="add_over_readers",
    )(index, got)


def finish_kernel(count, step, *refs):
    squares, (got_ref, key_ref, value_ref) = refs[:-3], refs[-3:]
    total = sum(jnp.sum(ref[...], axis=(0, 1), keepdims=True) for ref in squares)
    inv = 1.0 / jnp.sqrt(total / count + 1e-6)
    for m in range(got_ref.shape[0]):
        t, h, kind = m // 4, (m // 2) % 2, m % 2
        dst = (key_ref, value_ref)[kind]
        part = got_ref[m].astype(jnp.float32) * inv.reshape(1, 1, 1)
        dst[:, t * SLICE : (t + 1) * SLICE, h * HD : (h + 1) * HD] = part


def finish(squares, got, block_tok, width, count):
    slices, blocks = got.shape[0], got.shape[1] - 1
    step = 4
    shape = jax.ShapeDtypeStruct((blocks, block_tok, width), jnp.float32)
    spec = pl.BlockSpec((step, block_tok, width), lambda n: (n, 0, 0))
    return pl.pallas_call(
        functools.partial(finish_kernel, count, step),
        out_shape=(shape, shape),
        grid=(blocks // step,),
        in_specs=[pl.BlockSpec((8, HD), lambda n: (0, 0))] * len(squares)
        + [pl.BlockSpec((slices, step, SLICE, HD), lambda n: (0, n, 0, 0))],
        out_specs=(spec, spec),
        compiler_params=pltpu.CompilerParams(vmem_limit_bytes=24 * MIB),
        name="normalize_updates",
    )(*squares, got)


def swap(a):
    return lax.all_to_all(a, "wide", split_axis=0, concat_axis=0, tiled=True)


def local(
    queries,
    own_keys,
    own_values,
    cart_keys,
    cart_values,
    block_ids,
    block_home,
    query_len,
    grad_out,
):
    wide_count = lax.axis_size("wide")
    blk_dev, block_tok, width = cart_keys.shape
    selected = block_ids.shape[1]
    all_blocks = block_home.shape[0]
    held = swap(split(block_ids, block_home, cart_keys, cart_values, wide_count))
    asked = held[:, blk_dev, :2, :selected].astype(jnp.int32)
    owner, row = asked[:, 0], asked[:, 1]
    picked = pick(
        (owner * (blk_dev + 1) + row).reshape(-1),
        held.reshape(wide_count * (blk_dev + 1), SLICE, HD),
    )
    kv = swap(picked.reshape(wide_count, selected * SLICE, HD))
    attn_out, grad_queries, send = attend(
        query_len, kv, queries[0], grad_out[0], own_keys[0], own_values[0]
    )
    got = swap(send).reshape(wide_count, selected, SLICE, HD)
    back = swap(add_up(owner * blk_dev + row, got, blk_dev))
    squares = jnp.sum(
        back[:, blk_dev].astype(jnp.float32).reshape(2 * wide_count, SLICE // 2, HD), axis=0
    )
    mp = lax.axis_size("mp")
    shifts = [[(i, (i + d) % mp) for i in range(mp)] for d in range(1, mp)]
    squares = [squares] + [lax.ppermute(squares, "mp", pairs) for pairs in shifts]
    count = 2.0 * all_blocks * block_tok * width * mp
    key_update, value_update = finish(squares, back, block_tok, width, count)
    return (attn_out[None], grad_queries[None], key_update, value_update)


def solution(mesh):
    shared = P("wide", None, "mp")
    return jax.shard_map(
        local,
        mesh=mesh,
        in_specs=(shared, shared, shared, shared, shared, P("wide", None), P(), P("wide"), shared),
        out_specs=(shared, shared, shared, shared),
        check_vma=False,
    )
```

```python
import functools
import math

import jax
import jax.numpy as jnp
from jax import lax
from jax.experimental import pallas as pl
from jax.experimental.pallas import tpu as pltpu
from jax.sharding import PartitionSpec as P

HD = 128
HEADS = 2
KINDS = 2
MIB = 1024 * 1024

def nt(a, b):
    return lax.dot_general(a, b, (((1,), (1,)), ((), ())), preferred_element_type=jnp.float32)


def nn(a, b):
    return jnp.dot(a, b, preferred_element_type=jnp.float32)


def pack_kernel(asked_ref, keys_ref, values_ref, out_ref):
    def step(reader, carry):
        row = jnp.maximum(asked_ref[reader, 0, 0] - 1, 0)
        out_ref[reader, 0] = keys_ref[row]
        out_ref[reader, 1] = values_ref[row]
        return carry

    lax.fori_loop(0, out_ref.shape[0], step, 0)


def pack(asked, keys, values):
    vmem = pl.BlockSpec(memory_space=pltpu.VMEM)
    return pl.pallas_call(
        pack_kernel,
        out_shape=jax.ShapeDtypeStruct((asked.shape[0], KINDS) + keys.shape[1:], jnp.bfloat16),
        in_specs=[pl.BlockSpec(memory_space=pltpu.SMEM), vmem, vmem],
        out_specs=vmem,
        compiler_params=pltpu.CompilerParams(vmem_limit_bytes=16 * MIB),
        name="pack_slots",
    )(asked, keys, values)


def attend_kernel(
    length_ref,
    slot_ref,
    kv_ref,
    q_ref,
    g_ref,
    own_k_ref,
    own_v_ref,
    out_ref,
    grad_q_ref,
    send_ref,
    score,
    expo,
    acc,
    q_rows,
    g_cols,
):
    used = length_ref[0]
    chunks, chunk, _ = score.shape
    tokens = kv_ref.shape[2]
    pair = chunk // tokens
    rows = q_rows.shape[0]
    queries = q_ref.shape[0]
    repeat = rows // queries
    own = own_k_ref.shape[0]
    scale = 1.0 / math.sqrt(HD)
    log2e = scale * math.log2(math.e)
    position = lax.rem(lax.broadcasted_iota(jnp.int32, (1, rows), 1), queries)
    row_used = position < used
    own_at = lax.broadcasted_iota(jnp.int32, (own, rows), 0)
    seen = (own_at <= position) & (own_at < used)
    for head in range(HEADS):
        lanes = slice(head * HD, (head + 1) * HD)
        own_k = own_k_ref[:, lanes]
        own_v = own_v_ref[:, lanes]

        def read(c, kind):
            parts = [kv_ref[slot_ref[c * pair + n], kind, :, lanes] for n in range(pair)]
            return jnp.concatenate(parts, axis=0)

        def write(c, kind, value):
            for n in range(pair):
                part = value[n * tokens : (n + 1) * tokens].astype(jnp.bfloat16)
                send_ref[slot_ref[c * pair + n], kind, :, lanes] = part

        for r in range(repeat):
            cols = slice((head * repeat + r) * HD, (head * repeat + r + 1) * HD)
            q_rows[r * queries : (r + 1) * queries] = q_ref[:, cols]
            g_cols[:, r * queries : (r + 1) * queries] = g_ref[:, cols].T
        own_s = jnp.where(seen, nt(own_k, q_rows[...]), -1e30)
        top = jnp.max(own_s.reshape(own // 8, 8, rows), axis=0)
        for c in range(chunks):
            s = nt(read(c, 0), q_rows[...])
            score[c] = s
            top = jnp.maximum(top, jnp.max(s.reshape(chunk // 8, 8, rows), axis=0))
        top = jnp.max(top, axis=0, keepdims=True) * log2e
        e = jnp.exp2(own_s * log2e - top)
        total = jnp.sum(e.reshape(own // 8, 8, rows), axis=0)
        own_e = e.astype(jnp.bfloat16)
        acc[...] = nn(own_v.T, own_e)
        for c in range(chunks):
            e = jnp.exp2(score[c] * log2e - top)
            total = total + jnp.sum(e.reshape(chunk // 8, 8, rows), axis=0)
            low = e.astype(jnp.bfloat16)
            expo[c] = low
            acc[...] += nn(read(c, 1).T, low)
        inv = 1.0 / jnp.sum(total, axis=0, keepdims=True)
        g = jnp.where(row_used, g_cols[...].astype(jnp.float32), 0.0)
        out = jnp.where(row_used, acc[...] * inv, 0.0)
        for r in range(repeat):
            cols = slice((head * repeat + r) * HD, (head * repeat + r + 1) * HD)
            out_ref[:, cols] = out[:, r * queries : (r + 1) * queries].T.astype(jnp.bfloat16)
        delta = jnp.sum(g * out, axis=0, keepdims=True) * inv
        gs = (g * inv).astype(jnp.bfloat16)
        ds = (own_e.astype(jnp.float32) * (nn(own_v, gs) - delta)).astype(jnp.bfloat16)
        acc[...] = nn(own_k.T, ds)
        for c in range(chunks):
            low = expo[c]
            write(c, 1, nt(low, gs))
            dp = nn(read(c, 1), gs)
            ds = (low.astype(jnp.float32) * (dp - delta)).astype(jnp.bfloat16)
            write(c, 0, nn(ds, q_rows[...]) * scale)
            acc[...] += nn(read(c, 0).T, ds)
        grad = acc[...] * scale
        for r in range(repeat):
            cols = slice((head * repeat + r) * HD, (head * repeat + r + 1) * HD)
            grad_q_ref[:, cols] = grad[:, r * queries : (r + 1) * queries].T.astype(jnp.bfloat16)


def attend(length, slots, kv, q, g, own_k, own_v):
    chunk = 2 * kv.shape[2]
    queries, width = q.shape
    rows = queries * width // (HEADS * HD)
    chunks = slots.shape[0] * kv.shape[2] // chunk
    vmem = pl.BlockSpec(memory_space=pltpu.VMEM)
    return pl.pallas_call(
        attend_kernel,
        out_shape=(
            jax.ShapeDtypeStruct(q.shape, jnp.bfloat16),
            jax.ShapeDtypeStruct(q.shape, jnp.bfloat16),
            jax.ShapeDtypeStruct(kv.shape, jnp.bfloat16),
        ),
        in_specs=[pl.BlockSpec(memory_space=pltpu.SMEM)] * 2 + [vmem] * 5,
        out_specs=(vmem, vmem, vmem),
        scratch_shapes=[
            pltpu.VMEM((chunks, chunk, rows), jnp.float32),
            pltpu.VMEM((chunks, chunk, rows), jnp.bfloat16),
            pltpu.VMEM((HD, rows), jnp.float32),
            pltpu.VMEM((rows, HD), jnp.bfloat16),
            pltpu.VMEM((HD, rows), jnp.bfloat16),
        ],
        compiler_params=pltpu.CompilerParams(vmem_limit_bytes=44 * MIB),
        cost_estimate=pl.CostEstimate(
            flops=12 * 2 * HD * rows * (chunks * chunk + queries),
            bytes_accessed=8 * MIB,
            transcendentals=HEADS * rows * chunks * chunk,
        ),
        name="attend_forward_backward",
    )(length, slots, kv, q, g, own_k, own_v)


def add_kernel(asked_ref, got_ref, keys_ref, values_ref, squares_ref):
    sums = (keys_ref, values_ref)
    for ref in sums:
        ref[...] = jnp.zeros_like(ref)

    def step(reader, carry):
        asked = asked_ref[reader, 0, 0]

        @pl.when(asked > 0)
        def _():
            for kind, ref in enumerate(sums):
                ref[asked - 1] += got_ref[reader, kind].astype(jnp.float32)

        return carry

    lax.fori_loop(0, got_ref.shape[0], step, 0)
    blocks, tokens, width = keys_ref.shape

    def square(block, total):
        for ref in sums:
            rows = ref[block]
            total = total + jnp.sum((rows * rows).reshape(tokens // 8, 8, width), axis=0)
        return total

    total = lax.fori_loop(0, blocks, square, jnp.zeros((8, width), jnp.float32))
    total = jnp.sum(total, axis=0, keepdims=True)
    total = sum(total[:, n * HD : (n + 1) * HD] for n in range(width // HD))
    squares_ref[...] = jnp.broadcast_to(total[None], squares_ref.shape)


def add_up(asked, got, blocks, devices):
    vmem = pl.BlockSpec(memory_space=pltpu.VMEM)
    sums = jax.ShapeDtypeStruct((blocks,) + got.shape[2:], jnp.float32)
    return pl.pallas_call(
        add_kernel,
        out_shape=(sums, sums, jax.ShapeDtypeStruct((devices, 1, HD), jnp.float32)),
        in_specs=[pl.BlockSpec(memory_space=pltpu.SMEM), vmem],
        out_specs=(vmem, vmem, vmem),
        compiler_params=pltpu.CompilerParams(vmem_limit_bytes=24 * MIB),
        name="add_over_readers",
    )(asked, got)


def finish_kernel(count, squares_ref, keys_ref, values_ref, key_ref, value_ref):
    total = jnp.sum(jnp.sum(squares_ref[...], axis=0), axis=1, keepdims=True)
    inv = (1.0 / jnp.sqrt(total / count + 1e-6)).reshape(1, 1, 1)
    step = key_ref.shape[0]
    at = pl.ds(pl.program_id(0) * step, step)
    key_ref[...] = keys_ref[at] * inv
    value_ref[...] = values_ref[at] * inv


def finish(squares, keys, values, count):
    step = 2
    vmem = pl.BlockSpec(memory_space=pltpu.VMEM)
    shape = jax.ShapeDtypeStruct(keys.shape, jnp.float32)
    spec = pl.BlockSpec((step,) + keys.shape[1:], lambda n: (n, 0, 0))
    return pl.pallas_call(
        functools.partial(finish_kernel, count),
        out_shape=(shape, shape),
        grid=(keys.shape[0] // step,),
        in_specs=[vmem, vmem, vmem],
        out_specs=(spec, spec),
        compiler_params=pltpu.CompilerParams(vmem_limit_bytes=24 * MIB),
        name="normalize_updates",
    )(squares, keys, values)


def swap(a, axes="wide"):
    return lax.all_to_all(a, axes, split_axis=0, concat_axis=0, tiled=True)


def local(
    queries,
    own_keys,
    own_values,
    cart_keys,
    cart_values,
    block_ids,
    block_home,
    query_len,
    grad_out,
):
    wide_count, mp = lax.axis_size("wide"), lax.axis_size("mp")
    blk_dev = cart_keys.shape[0]
    lookup = block_ids[0][:, None] == jnp.arange(block_home.shape[0], dtype=jnp.int32)
    storage = jnp.sum(jnp.where(lookup, block_home[None, :], 0), axis=-1)
    slots, row = storage // blk_dev, storage % blk_dev
    mine = slots[None, :] == jnp.arange(wide_count, dtype=jnp.int32)[:, None]
    ask = jnp.sum(jnp.where(mine, row[None, :] + 1, 0), axis=1)
    asked = swap(jnp.broadcast_to(ask[:, None, None], (wide_count, 1, HD)))
    kv = swap(pack(asked, cart_keys, cart_values))
    attn_out, grad_queries, send = attend(
        query_len, slots, kv, queries[0], grad_out[0], own_keys[0], own_values[0]
    )
    keys, values, squares = add_up(asked, swap(send), blk_dev, wide_count * mp)
    squares = swap(squares, ("wide", "mp"))
    count = 2.0 * keys.size * wide_count * mp
    key_update, value_update = finish(squares, keys, values, count)
    return (attn_out[None], grad_queries[None], key_update, value_update)


def solution(mesh):
    shared = P("wide", None, "mp")
    return jax.shard_map(
        local,
        mesh=mesh,
        in_specs=(shared, shared, shared, shared, shared, P("wide", None), P(), P("wide"), shared),
        out_specs=(shared, shared, shared, shared),
        check_vma=False,
    )
```

```python
import functools
import math

import jax
import jax.numpy as jnp
from jax import lax
from jax.experimental import pallas as pl
from jax.experimental.pallas import tpu as pltpu
from jax.sharding import PartitionSpec as P

HD = 128
SLICE = 16
TAG = 8
HEADS = 2
KINDS = 2
MIB = 1024 * 1024


def nt(a, b):
    return lax.dot_general(a, b, (((1,), (1,)), ((), ())), preferred_element_type=jnp.float32)


def nn(a, b):
    return jnp.dot(a, b, preferred_element_type=jnp.float32)


def split_kernel(
    ids_ref,
    home_ref,
    length_ref,
    keys_ref,
    values_ref,
    out_ref,
    used_ref,
    inside,
    parts,
    ids,
    home,
    length,
    in_sems,
    out_sems,
    list_sems,
):
    blocks, tokens, width = keys_ref.shape
    groups = tokens // SLICE
    arrive = []
    for t in range(groups):
        for kind, src in enumerate((keys_ref, values_ref)):
            copy = pltpu.make_async_copy(
                src.at[:, pl.ds(t * SLICE, SLICE)], inside.at[t, kind], in_sems.at[t, kind]
            )
            copy.start()
            arrive.append(copy)
    lists = ((ids_ref, ids), (home_ref, home), (length_ref, length))
    lists = [
        pltpu.make_async_copy(src, dst, list_sems.at[n]) for n, (src, dst) in enumerate(lists)
    ]
    for copy in lists:
        copy.start()
    for copy in lists:
        copy.wait()
    used_ref[...] = jnp.full(used_ref.shape, length[0], jnp.int32)
    line = lax.broadcasted_iota(jnp.int32, (SLICE, HD), 0)
    lane = lax.broadcasted_iota(jnp.int32, (SLICE, HD), 1)
    tag = jnp.zeros((SLICE, HD), jnp.int32)
    for k in range(ids.shape[1]):
        storage = home[ids[0, k]]
        owner = lax.div(storage, blocks)
        tag = jnp.where((line == 0) & (lane == k), owner, tag)
        tag = jnp.where((line == 1) & (lane == k), storage - owner * blocks, tag)
    tag = tag.astype(jnp.float32).astype(jnp.bfloat16)
    leave = []
    for t in range(groups):
        for kind in range(KINDS):
            arrive[t * KINDS + kind].wait()
        for part in range(HEADS * KINDS):
            m = t * HEADS * KINDS + part
            h, kind = part // KINDS, part % KINDS
            parts[m, pl.ds(0, blocks)] = inside[t, kind, :, :, h * HD : (h + 1) * HD]
            parts[m, blocks] = tag
            copy = pltpu.make_async_copy(parts.at[m], out_ref.at[m], out_sems.at[m])
            copy.start()
            leave.append(copy)
    for copy in leave:
        copy.wait()


def split(block_ids, block_home, length, cart_keys, cart_values, count):
    blocks, tokens, width = cart_keys.shape
    groups = tokens // SLICE
    hbm = pl.BlockSpec(memory_space=pltpu.HBM)
    return pl.pallas_call(
        split_kernel,
        out_shape=(
            jax.ShapeDtypeStruct((count, blocks + 1, SLICE, HD), jnp.bfloat16),
            jax.ShapeDtypeStruct((8, HD), jnp.int32),
        ),
        in_specs=[hbm] * 5,
        out_specs=(hbm, pl.BlockSpec(memory_space=pltpu.VMEM)),
        scratch_shapes=[
            pltpu.VMEM((groups, KINDS, blocks, SLICE, width), jnp.bfloat16),
            pltpu.VMEM((count, blocks + 1, SLICE, HD), jnp.bfloat16),
            pltpu.SMEM(block_ids.shape, jnp.int32),
            pltpu.SMEM(block_home.shape, jnp.int32),
            pltpu.SMEM(length.shape, jnp.int32),
            pltpu.SemaphoreType.DMA((groups, KINDS)),
            pltpu.SemaphoreType.DMA((count,)),
            pltpu.SemaphoreType.DMA((3,)),
        ],
        name="split_blocks",
    )(block_ids, block_home, length, cart_keys, cart_values)


def pick_kernel(index_ref, held_ref, out_ref):
    def step(n, carry):
        for u in range(16):
            out_ref[n * 16 + u] = held_ref[index_ref[n * 16 + u]]
        return carry

    lax.fori_loop(0, out_ref.shape[0] // 16, step, 0)


def pick(index, held):
    vmem = pl.BlockSpec(memory_space=pltpu.VMEM)
    return pl.pallas_call(
        pick_kernel,
        out_shape=jax.ShapeDtypeStruct((index.shape[0],) + held.shape[1:], jnp.bfloat16),
        in_specs=[pl.BlockSpec(memory_space=pltpu.SMEM), vmem],
        out_specs=vmem,
        compiler_params=pltpu.CompilerParams(vmem_limit_bytes=16 * MIB),
        name="pick_requested",
    )(index, held)


def attend_kernel(
    length_ref,
    kv_ref,
    q_ref,
    g_ref,
    own_k_ref,
    own_v_ref,
    out_ref,
    grad_q_ref,
    send_ref,
    score,
    expo,
    acc,
    q_rows,
    g_cols,
):
    used = length_ref[0:1, 0:1]
    chunks = kv_ref.shape[0] // (HEADS * KINDS)
    chunk = kv_ref.shape[1]
    rows = q_rows.shape[0]
    queries = q_ref.shape[0]
    repeat = rows // queries
    own = own_k_ref.shape[0]
    scale = 1.0 / math.sqrt(HD)
    log2e = scale * math.log2(math.e)
    position = lax.rem(lax.broadcasted_iota(jnp.int32, (1, rows), 1), queries)
    row_used = position < used
    own_at = lax.broadcasted_iota(jnp.int32, (own, rows), 0)
    seen = (own_at <= position) & (own_at < used)
    for head in range(HEADS):
        lanes = slice(head * HD, (head + 1) * HD)
        own_k = own_k_ref[:, lanes]
        own_v = own_v_ref[:, lanes]
        at = lambda c, kind: (c * HEADS + head) * KINDS + kind
        for r in range(repeat):
            cols = slice((head * repeat + r) * HD, (head * repeat + r + 1) * HD)
            q_rows[r * queries : (r + 1) * queries] = q_ref[:, cols]
            g_cols[:, r * queries : (r + 1) * queries] = g_ref[:, cols].T
        own_s = jnp.where(seen, nt(own_k, q_rows[...]), -1e30)
        top = jnp.max(own_s.reshape(own // 8, 8, rows), axis=0)
        for c in range(chunks):
            s = nt(kv_ref[at(c, 0)], q_rows[...])
            score[c] = s
            top = jnp.maximum(top, jnp.max(s.reshape(chunk // 8, 8, rows), axis=0))
        top = jnp.max(top, axis=0, keepdims=True) * log2e
        e = jnp.exp2(own_s * log2e - top)
        total = jnp.sum(e.reshape(own // 8, 8, rows), axis=0)
        own_e = e.astype(jnp.bfloat16)
        acc[...] = nn(own_v.T, own_e)
        for c in range(chunks):
            e = jnp.exp2(score[c] * log2e - top)
            total = total + jnp.sum(e.reshape(chunk // 8, 8, rows), axis=0)
            low = e.astype(jnp.bfloat16)
            expo[c] = low
            acc[...] += nn(kv_ref[at(c, 1)].T, low)
        inv = 1.0 / jnp.sum(total, axis=0, keepdims=True)
        g = jnp.where(row_used, g_cols[...].astype(jnp.float32), 0.0)
        out = jnp.where(row_used, acc[...] * inv, 0.0)
        for r in range(repeat):
            cols = slice((head * repeat + r) * HD, (head * repeat + r + 1) * HD)
            out_ref[:, cols] = out[:, r * queries : (r + 1) * queries].T.astype(jnp.bfloat16)
        delta = jnp.sum(g * out, axis=0, keepdims=True) * inv
        gs = (g * inv).astype(jnp.bfloat16)
        ds = (own_e.astype(jnp.float32) * (nn(own_v, gs) - delta)).astype(jnp.bfloat16)
        acc[...] = nn(own_k.T, ds)
        for c in range(chunks):
            low = expo[c]
            send_ref[at(c, 1)] = nt(low, gs).astype(jnp.bfloat16)
            dp = nn(kv_ref[at(c, 1)], gs)
            ds = (low.astype(jnp.float32) * (dp - delta)).astype(jnp.bfloat16)
            send_ref[at(c, 0)] = (nn(ds, q_rows[...]) * scale).astype(jnp.bfloat16)
            acc[...] += nn(kv_ref[at(c, 0)].T, ds)
        grad = acc[...] * scale
        for r in range(repeat):
            cols = slice((head * repeat + r) * HD, (head * repeat + r + 1) * HD)
            grad_q_ref[:, cols] = grad[:, r * queries : (r + 1) * queries].T.astype(jnp.bfloat16)


def attend(length, kv, q, g, own_k, own_v):
    count, chunk, _ = kv.shape
    queries, width = q.shape
    rows = queries * width // (HEADS * HD)
    chunks = count // (HEADS * KINDS)
    vmem = pl.BlockSpec(memory_space=pltpu.VMEM)
    return pl.pallas_call(
        attend_kernel,
        out_shape=(
            jax.ShapeDtypeStruct(q.shape, jnp.bfloat16),
            jax.ShapeDtypeStruct(q.shape, jnp.bfloat16),
            jax.ShapeDtypeStruct(kv.shape, jnp.bfloat16),
        ),
        in_specs=[vmem] * 6,
        out_specs=(vmem, vmem, vmem),
        scratch_shapes=[
            pltpu.VMEM((chunks, chunk, rows), jnp.float32),
            pltpu.VMEM((chunks, chunk, rows), jnp.bfloat16),
            pltpu.VMEM((HD, rows), jnp.float32),
            pltpu.VMEM((rows, HD), jnp.bfloat16),
            pltpu.VMEM((HD, rows), jnp.bfloat16),
        ],
        compiler_params=pltpu.CompilerParams(vmem_limit_bytes=48 * MIB),
        cost_estimate=pl.CostEstimate(
            flops=12 * 2 * HD * rows * (chunks * chunk + queries),
            bytes_accessed=8 * MIB,
            transcendentals=HEADS * rows * chunks * chunk,
        ),
        name="attend_forward_backward",
    )(length, kv, q, g, own_k, own_v)


def add_kernel(index_ref, got_ref, out_ref, table):
    selected = index_ref.shape[1]
    owners, held = out_ref.shape[0], out_ref.shape[1] - TAG
    blocks = held // SLICE
    table[...] = jnp.zeros_like(table)

    def step(n, carry):
        at = [index_ref[n, k] for k in range(selected)]
        sums = [table[at[k]] + got_ref[n, k].astype(jnp.float32) for k in range(selected)]
        for k in range(selected):
            table[at[k]] = sums[k]
        return carry

    lax.fori_loop(0, got_ref.shape[0], step, 0, unroll=4)

    def finish(n, squares):
        rows = table[pl.ds(n * blocks, blocks)].reshape(held, HD)
        out_ref[n, pl.ds(0, held)] = rows.astype(jnp.bfloat16)
        return squares + jnp.sum((rows * rows).reshape(held // 8, 8, HD), axis=0)

    squares = lax.fori_loop(0, owners, finish, jnp.zeros((8, HD), jnp.float32), unroll=4)
    squares = squares[: TAG // 2] + squares[TAG // 2 :]
    high = squares.astype(jnp.bfloat16).astype(jnp.float32)
    tag = jnp.concatenate([high, squares - high], axis=0).astype(jnp.bfloat16)
    for n in range(owners):
        out_ref[n, pl.ds(held, TAG)] = tag


def add_up(index, got, blk_dev):
    count = got.shape[0]
    vmem = pl.BlockSpec(memory_space=pltpu.VMEM)
    return pl.pallas_call(
        add_kernel,
        out_shape=jax.ShapeDtypeStruct((count, blk_dev * SLICE + TAG, HD), jnp.bfloat16),
        in_specs=[pl.BlockSpec(memory_space=pltpu.SMEM), vmem],
        out_specs=vmem,
        scratch_shapes=[pltpu.VMEM((count * blk_dev, SLICE, HD), jnp.float32)],
        compiler_params=pltpu.CompilerParams(vmem_limit_bytes=24 * MIB),
        name="add_over_readers",
    )(index, got)


def finish_kernel(count, *refs):
    squares, (got_ref, key_ref, value_ref, keys, values, sems) = refs[:-6], refs[-6:]
    total = jnp.sum(sum(ref[...] for ref in squares), axis=(0, 1), keepdims=True)
    inv = 1.0 / jnp.sqrt(total / count + 1e-6)
    parts = sems.shape[0]
    step = keys.shape[0] // parts
    copies = []
    for n in range(parts):
        at = pl.ds(n * step, step)
        for m in range(got_ref.shape[0]):
            t, h, kind = m // 4, (m // 2) % 2, m % 2
            part = got_ref[m, n * step * SLICE : (n + 1) * step * SLICE].astype(jnp.float32) * inv
            part = part.reshape(step, SLICE, HD)
            (keys, values)[kind][at, t * SLICE : (t + 1) * SLICE, h * HD : (h + 1) * HD] = part
        for kind, (src, dst) in enumerate(((keys, key_ref), (values, value_ref))):
            copies.append(pltpu.make_async_copy(src.at[at], dst.at[at], sems.at[n, kind]))
            copies[-1].start()
    for copy in copies:
        copy.wait()


def finish(squares, got, block_tok, width, count):
    blocks = (got.shape[1] - TAG) // SLICE
    vmem = pl.BlockSpec(memory_space=pltpu.VMEM)
    hbm = pl.BlockSpec(memory_space=pltpu.HBM)
    shape = (blocks, block_tok, width)
    return pl.pallas_call(
        functools.partial(finish_kernel, count),
        out_shape=(jax.ShapeDtypeStruct(shape, jnp.float32),) * 2,
        in_specs=[vmem] * (len(squares) + 1),
        out_specs=(hbm, hbm),
        scratch_shapes=[
            pltpu.VMEM(shape, jnp.float32),
            pltpu.VMEM(shape, jnp.float32),
            pltpu.SemaphoreType.DMA((4, KINDS)),
        ],
        compiler_params=pltpu.CompilerParams(vmem_limit_bytes=24 * MIB),
        name="normalize_updates",
    )(*squares, got)


def swap(a):
    return lax.all_to_all(a, "wide", split_axis=0, concat_axis=0, tiled=True)


def local(
    queries,
    own_keys,
    own_values,
    cart_keys,
    cart_values,
    block_ids,
    block_home,
    query_len,
    grad_out,
):
    wide_count = lax.axis_size("wide")
    blk_dev, block_tok, width = cart_keys.shape
    selected = block_ids.shape[1]
    all_blocks = block_home.shape[0]
    parts, used = split(block_ids, block_home, query_len, cart_keys, cart_values, wide_count)
    held = swap(parts)
    asked = held[:, blk_dev, :2, :selected].astype(jnp.int32)
    owner, row = asked[:, 0], asked[:, 1]
    picked = pick(
        (owner * (blk_dev + 1) + row).reshape(-1),
        held.reshape(wide_count * (blk_dev + 1), SLICE, HD),
    )
    kv = swap(picked.reshape(wide_count, selected * SLICE, HD))
    attn_out, grad_queries, send = attend(
        used, kv, queries[0], grad_out[0], own_keys[0], own_values[0]
    )
    got = swap(send).reshape(wide_count, selected, SLICE, HD)
    back = swap(add_up(owner * blk_dev + row, got, blk_dev))
    squares = jnp.sum(back[:, -TAG:].astype(jnp.float32), axis=0)
    mp = lax.axis_size("mp")
    shifts = [[(i, (i + d) % mp) for i in range(mp)] for d in range(1, mp)]
    squares = [squares] + [lax.ppermute(squares, "mp", pairs) for pairs in shifts]
    count = 2.0 * all_blocks * block_tok * width * mp
    key_update, value_update = finish(squares, back, block_tok, width, count)
    return (attn_out[None], grad_queries[None], key_update, value_update)


def solution(mesh):
    shared = P("wide", None, "mp")
    return jax.shard_map(
        local,
        mesh=mesh,
        in_specs=(shared, shared, shared, shared, shared, P("wide", None), P(), P("wide"), shared),
        out_specs=(shared, shared, shared, shared),
        check_vma=False,
    )
```

```python
import functools
import math

import jax
import jax.numpy as jnp
from jax import lax
from jax.experimental import pallas as pl
from jax.experimental.pallas import tpu as pltpu
from jax.sharding import PartitionSpec as P

HD = 128
SLICE = 16
TAG = 8
HEADS = 2
KINDS = 2
MIB = 1024 * 1024


def nt(a, b):
    return lax.dot_general(a, b, (((1,), (1,)), ((), ())), preferred_element_type=jnp.float32)


def nn(a, b):
    return jnp.dot(a, b, preferred_element_type=jnp.float32)


def split_kernel(
    ids_ref,
    home_ref,
    length_ref,
    keys_ref,
    values_ref,
    out_ref,
    used_ref,
    inside,
    parts,
    ids,
    home,
    length,
    in_sems,
    out_sems,
    list_sems,
):
    blocks, tokens, width = keys_ref.shape
    groups = tokens // SLICE
    arrive = []
    for t in range(groups):
        for kind, src in enumerate((keys_ref, values_ref)):
            copy = pltpu.make_async_copy(
                src.at[:, pl.ds(t * SLICE, SLICE)], inside.at[t, kind], in_sems.at[t, kind]
            )
            copy.start()
            arrive.append(copy)
    lists = ((ids_ref, ids), (home_ref, home), (length_ref, length))
    lists = [
        pltpu.make_async_copy(src, dst, list_sems.at[n]) for n, (src, dst) in enumerate(lists)
    ]
    for copy in lists:
        copy.start()
    for copy in lists:
        copy.wait()
    used_ref[...] = jnp.full(used_ref.shape, length[0], jnp.int32)
    line = lax.broadcasted_iota(jnp.int32, (SLICE, HD), 0)
    lane = lax.broadcasted_iota(jnp.int32, (SLICE, HD), 1)
    tag = jnp.zeros((SLICE, HD), jnp.int32)
    for k in range(ids.shape[1]):
        storage = home[ids[0, k]]
        owner = lax.div(storage, blocks)
        tag = jnp.where((line == 0) & (lane == k), owner, tag)
        tag = jnp.where((line == 1) & (lane == k), storage - owner * blocks, tag)
    tag = tag.astype(jnp.float32).astype(jnp.bfloat16)
    leave = []
    for t in range(groups):
        for kind in range(KINDS):
            arrive[t * KINDS + kind].wait()
        for part in range(HEADS * KINDS):
            m = t * HEADS * KINDS + part
            h, kind = part // KINDS, part % KINDS
            parts[m, pl.ds(0, blocks)] = inside[t, kind, :, :, h * HD : (h + 1) * HD]
            parts[m, blocks] = tag
            copy = pltpu.make_async_copy(parts.at[m], out_ref.at[m], out_sems.at[m])
            copy.start()
            leave.append(copy)
    for copy in leave:
        copy.wait()


def split(block_ids, block_home, length, cart_keys, cart_values, count):
    blocks, tokens, width = cart_keys.shape
    groups = tokens // SLICE
    hbm = pl.BlockSpec(memory_space=pltpu.HBM)
    return pl.pallas_call(
        split_kernel,
        out_shape=(
            jax.ShapeDtypeStruct((count, blocks + 1, SLICE, HD), jnp.bfloat16),
            jax.ShapeDtypeStruct((8, HD), jnp.int32),
        ),
        in_specs=[hbm] * 5,
        out_specs=(hbm, pl.BlockSpec(memory_space=pltpu.VMEM)),
        scratch_shapes=[
            pltpu.VMEM((groups, KINDS, blocks, SLICE, width), jnp.bfloat16),
            pltpu.VMEM((count, blocks + 1, SLICE, HD), jnp.bfloat16),
            pltpu.SMEM(block_ids.shape, jnp.int32),
            pltpu.SMEM(block_home.shape, jnp.int32),
            pltpu.SMEM(length.shape, jnp.int32),
            pltpu.SemaphoreType.DMA((groups, KINDS)),
            pltpu.SemaphoreType.DMA((count,)),
            pltpu.SemaphoreType.DMA((3,)),
        ],
        name="split_blocks",
    )(block_ids, block_home, length, cart_keys, cart_values)


def pick_kernel(index_ref, held_ref, out_ref):
    def step(n, carry):
        for u in range(16):
            out_ref[n * 16 + u] = held_ref[index_ref[n * 16 + u]]
        return carry

    lax.fori_loop(0, out_ref.shape[0] // 16, step, 0)


def pick(index, held):
    vmem = pl.BlockSpec(memory_space=pltpu.VMEM)
    return pl.pallas_call(
        pick_kernel,
        out_shape=jax.ShapeDtypeStruct((index.shape[0],) + held.shape[1:], jnp.bfloat16),
        in_specs=[pl.BlockSpec(memory_space=pltpu.SMEM), vmem],
        out_specs=vmem,
        compiler_params=pltpu.CompilerParams(vmem_limit_bytes=16 * MIB),
        name="pick_requested",
    )(index, held)


def attend_kernel(
    length_ref,
    kv_ref,
    q_ref,
    g_ref,
    own_k_ref,
    own_v_ref,
    send_ref,
    out_ref,
    slope_ref,
    own_slope_ref,
    score,
    expo,
    acc,
    q_rows,
    g_cols,
):
    used = length_ref[0:1, 0:1]
    chunks = kv_ref.shape[0] // (HEADS * KINDS)
    chunk = kv_ref.shape[1]
    rows = q_rows.shape[0]
    queries = q_ref.shape[0]
    repeat = rows // queries
    own = own_k_ref.shape[0]
    scale = 1.0 / math.sqrt(HD)
    log2e = scale * math.log2(math.e)
    position = lax.rem(lax.broadcasted_iota(jnp.int32, (1, rows), 1), queries)
    row_used = position < used
    own_at = lax.broadcasted_iota(jnp.int32, (own, rows), 0)
    seen = (own_at <= position) & (own_at < used)
    for head in range(HEADS):
        lanes = slice(head * HD, (head + 1) * HD)
        own_k = own_k_ref[:, lanes]
        own_v = own_v_ref[:, lanes]
        at = lambda c, kind: (c * HEADS + head) * KINDS + kind
        for r in range(repeat):
            cols = slice((head * repeat + r) * HD, (head * repeat + r + 1) * HD)
            q_rows[r * queries : (r + 1) * queries] = q_ref[:, cols]
            g_cols[:, r * queries : (r + 1) * queries] = g_ref[:, cols].T
        own_s = jnp.where(seen, nt(own_k, q_rows[...]), -1e30)
        top = jnp.max(own_s.reshape(own // 8, 8, rows), axis=0)
        for c in range(chunks):
            s = nt(kv_ref[at(c, 0)], q_rows[...])
            score[c] = s
            top = jnp.maximum(top, jnp.max(s.reshape(chunk // 8, 8, rows), axis=0))
        top = jnp.max(top, axis=0, keepdims=True) * log2e
        e = jnp.exp2(own_s * log2e - top)
        total = jnp.sum(e.reshape(own // 8, 8, rows), axis=0)
        own_e = e.astype(jnp.bfloat16)
        acc[...] = nn(own_v.T, own_e)
        for c in range(chunks):
            e = jnp.exp2(score[c] * log2e - top)
            total = total + jnp.sum(e.reshape(chunk // 8, 8, rows), axis=0)
            low = e.astype(jnp.bfloat16)
            expo[c] = low
            acc[...] += nn(kv_ref[at(c, 1)].T, low)
        inv = 1.0 / jnp.sum(total, axis=0, keepdims=True)
        g = jnp.where(row_used, g_cols[...].astype(jnp.float32), 0.0)
        out = jnp.where(row_used, acc[...] * inv, 0.0)
        out_ref[head] = out
        delta = jnp.sum(g * out, axis=0, keepdims=True) * inv
        gs = (g * inv).astype(jnp.bfloat16)
        ds = own_e.astype(jnp.float32) * (nn(own_v, gs) - delta)
        own_slope_ref[head] = ds.astype(jnp.bfloat16)
        for c in range(chunks):
            low = expo[c]
            send_ref[at(c, 1)] = nt(low, gs).astype(jnp.bfloat16)
            dp = nn(kv_ref[at(c, 1)], gs)
            ds = (low.astype(jnp.float32) * (dp - delta)).astype(jnp.bfloat16)
            slope_ref[head, c] = ds
            send_ref[at(c, 0)] = (nn(ds, q_rows[...]) * scale).astype(jnp.bfloat16)


def attend(length, kv, q, g, own_k, own_v):
    count, chunk, _ = kv.shape
    queries, width = q.shape
    rows = queries * width // (HEADS * HD)
    chunks = count // (HEADS * KINDS)
    vmem = pl.BlockSpec(memory_space=pltpu.VMEM)
    return pl.pallas_call(
        attend_kernel,
        out_shape=(
            jax.ShapeDtypeStruct(kv.shape, jnp.bfloat16),
            jax.ShapeDtypeStruct((HEADS, HD, rows), jnp.float32),
            jax.ShapeDtypeStruct((HEADS, chunks, chunk, rows), jnp.bfloat16),
            jax.ShapeDtypeStruct((HEADS, own_k.shape[0], rows), jnp.bfloat16),
        ),
        in_specs=[vmem] * 6,
        out_specs=(vmem,) * 4,
        scratch_shapes=[
            pltpu.VMEM((chunks, chunk, rows), jnp.float32),
            pltpu.VMEM((chunks, chunk, rows), jnp.bfloat16),
            pltpu.VMEM((HD, rows), jnp.float32),
            pltpu.VMEM((rows, HD), jnp.bfloat16),
            pltpu.VMEM((HD, rows), jnp.bfloat16),
        ],
        compiler_params=pltpu.CompilerParams(vmem_limit_bytes=36 * MIB),
        cost_estimate=pl.CostEstimate(
            flops=10 * 2 * HD * rows * (chunks * chunk + queries),
            bytes_accessed=8 * MIB,
            transcendentals=HEADS * rows * chunks * chunk,
        ),
        name="attend_forward_backward",
    )(length, kv, q, g, own_k, own_v)


def rows_kernel(kv_ref, own_k_ref, out_t_ref, slope_ref, own_slope_ref, out_ref, grad_q_ref):
    chunks = slope_ref.shape[1]
    rows = out_t_ref.shape[2]
    queries = out_ref.shape[0]
    repeat = rows // queries
    scale = 1.0 / math.sqrt(HD)
    for head in range(HEADS):
        own_k = own_k_ref[:, head * HD : (head + 1) * HD]
        grad = nn(own_k.T, own_slope_ref[head])
        for c in range(chunks):
            grad += nn(kv_ref[(c * HEADS + head) * KINDS].T, slope_ref[head, c])
        grad = grad * scale
        out = out_t_ref[head]
        for r in range(repeat):
            cols = slice((head * repeat + r) * HD, (head * repeat + r + 1) * HD)
            at = slice(r * queries, (r + 1) * queries)
            out_ref[:, cols] = out[:, at].T.astype(jnp.bfloat16)
            grad_q_ref[:, cols] = grad[:, at].T.astype(jnp.bfloat16)


def query_rows(kv, own_k, out_t, slope, own_slope, queries, width):
    vmem = pl.BlockSpec(memory_space=pltpu.VMEM)
    shape = jax.ShapeDtypeStruct((queries, width), jnp.bfloat16)
    return pl.pallas_call(
        rows_kernel,
        out_shape=(shape, shape),
        in_specs=[vmem] * 5,
        out_specs=(vmem, vmem),
        compiler_params=pltpu.CompilerParams(vmem_limit_bytes=24 * MIB),
        cost_estimate=pl.CostEstimate(
            flops=2 * HD * HEADS * out_t.shape[2] * kv.shape[0] * kv.shape[1] // 2,
            bytes_accessed=12 * MIB,
            transcendentals=0,
        ),
        name="outputs_by_query",
    )(kv, own_k, out_t, slope, own_slope)


def add_kernel(index_ref, got_ref, out_ref, table):
    selected = index_ref.shape[1]
    owners, held = out_ref.shape[0], out_ref.shape[1] - TAG
    blocks = held // SLICE
    table[...] = jnp.zeros_like(table)

    def step(n, carry):
        at = [index_ref[n, k] for k in range(selected)]
        sums = [table[at[k]] + got_ref[n, k].astype(jnp.float32) for k in range(selected)]
        for k in range(selected):
            table[at[k]] = sums[k]
        return carry

    lax.fori_loop(0, got_ref.shape[0], step, 0, unroll=4)

    def finish(n, squares):
        rows = table[pl.ds(n * blocks, blocks)].reshape(held, HD)
        out_ref[n, pl.ds(0, held)] = rows.astype(jnp.bfloat16)
        return squares + jnp.sum((rows * rows).reshape(held // 8, 8, HD), axis=0)

    squares = lax.fori_loop(0, owners, finish, jnp.zeros((8, HD), jnp.float32), unroll=4)
    squares = squares[: TAG // 2] + squares[TAG // 2 :]
    high = squares.astype(jnp.bfloat16).astype(jnp.float32)
    tag = jnp.concatenate([high, squares - high], axis=0).astype(jnp.bfloat16)
    for n in range(owners):
        out_ref[n, pl.ds(held, TAG)] = tag


def add_up(index, got, blk_dev):
    count = got.shape[0]
    vmem = pl.BlockSpec(memory_space=pltpu.VMEM)
    return pl.pallas_call(
        add_kernel,
        out_shape=jax.ShapeDtypeStruct((count, blk_dev * SLICE + TAG, HD), jnp.bfloat16),
        in_specs=[pl.BlockSpec(memory_space=pltpu.SMEM), vmem],
        out_specs=vmem,
        scratch_shapes=[pltpu.VMEM((count * blk_dev, SLICE, HD), jnp.float32)],
        compiler_params=pltpu.CompilerParams(vmem_limit_bytes=24 * MIB),
        name="add_over_readers",
    )(index, got)


def finish_kernel(count, *refs):
    squares, (got_ref, key_ref, value_ref, keys, values, sems) = refs[:-6], refs[-6:]
    total = jnp.sum(sum(ref[...] for ref in squares), axis=(0, 1), keepdims=True)
    inv = 1.0 / jnp.sqrt(total / count + 1e-6)
    parts = sems.shape[0]
    step = keys.shape[0] // parts
    copies = []
    for n in range(parts):
        at = pl.ds(n * step, step)
        for m in range(got_ref.shape[0]):
            t, h, kind = m // 4, (m // 2) % 2, m % 2
            part = got_ref[m, n * step * SLICE : (n + 1) * step * SLICE].astype(jnp.float32) * inv
            part = part.reshape(step, SLICE, HD)
            (keys, values)[kind][at, t * SLICE : (t + 1) * SLICE, h * HD : (h + 1) * HD] = part
        for kind, (src, dst) in enumerate(((keys, key_ref), (values, value_ref))):
            copies.append(pltpu.make_async_copy(src.at[at], dst.at[at], sems.at[n, kind]))
            copies[-1].start()
    for copy in copies:
        copy.wait()


def finish(squares, got, block_tok, width, count):
    blocks = (got.shape[1] - TAG) // SLICE
    vmem = pl.BlockSpec(memory_space=pltpu.VMEM)
    hbm = pl.BlockSpec(memory_space=pltpu.HBM)
    shape = (blocks, block_tok, width)
    return pl.pallas_call(
        functools.partial(finish_kernel, count),
        out_shape=(jax.ShapeDtypeStruct(shape, jnp.float32),) * 2,
        in_specs=[vmem] * (len(squares) + 1),
        out_specs=(hbm, hbm),
        scratch_shapes=[
            pltpu.VMEM(shape, jnp.float32),
            pltpu.VMEM(shape, jnp.float32),
            pltpu.SemaphoreType.DMA((4, KINDS)),
        ],
        compiler_params=pltpu.CompilerParams(vmem_limit_bytes=24 * MIB),
        name="normalize_updates",
    )(*squares, got)


def swap(a):
    return lax.all_to_all(a, "wide", split_axis=0, concat_axis=0, tiled=True)


def local(
    queries,
    own_keys,
    own_values,
    cart_keys,
    cart_values,
    block_ids,
    block_home,
    query_len,
    grad_out,
):
    wide_count = lax.axis_size("wide")
    blk_dev, block_tok, width = cart_keys.shape
    selected = block_ids.shape[1]
    all_blocks = block_home.shape[0]
    parts, used = split(block_ids, block_home, query_len, cart_keys, cart_values, wide_count)
    held = swap(parts)
    asked = held[:, blk_dev, :2, :selected].astype(jnp.int32)
    owner, row = asked[:, 0], asked[:, 1]
    picked = pick(
        (owner * (blk_dev + 1) + row).reshape(-1),
        held.reshape(wide_count * (blk_dev + 1), SLICE, HD),
    )
    kv = swap(picked.reshape(wide_count, selected * SLICE, HD))
    send, out_t, slope, own_slope = attend(
        used, kv, queries[0], grad_out[0], own_keys[0], own_values[0]
    )
    got = swap(send).reshape(wide_count, selected, SLICE, HD)
    back = swap(add_up(owner * blk_dev + row, got, blk_dev))
    squares = jnp.sum(back[:, -TAG:].astype(jnp.float32), axis=0)
    mp = lax.axis_size("mp")
    shifts = [[(i, (i + d) % mp) for i in range(mp)] for d in range(1, mp)]
    squares = [squares] + [lax.ppermute(squares, "mp", pairs) for pairs in shifts]
    out_t, slope, _ = lax.optimization_barrier((out_t, slope, back))
    attn_out, grad_queries = query_rows(
        kv, own_keys[0], out_t, slope, own_slope, queries.shape[1], queries.shape[2]
    )
    count = 2.0 * all_blocks * block_tok * width * mp
    key_update, value_update = finish(squares, back, block_tok, width, count)
    return (attn_out[None], grad_queries[None], key_update, value_update)


def solution(mesh):
    shared = P("wide", None, "mp")
    return jax.shard_map(
        local,
        mesh=mesh,
        in_specs=(shared, shared, shared, shared, shared, P("wide", None), P(), P("wide"), shared),
        out_specs=(shared, shared, shared, shared),
        check_vma=False,
    )
```

```python
import functools
import math

import jax
import jax.numpy as jnp
from jax import lax
from jax.experimental import pallas as pl
from jax.experimental.pallas import tpu as pltpu
from jax.sharding import PartitionSpec as P

HD = 128
SLICE = 16
TAG = 8
HEADS = 2
KINDS = 2
MIB = 1024 * 1024


def nt(a, b):
    return lax.dot_general(a, b, (((1,), (1,)), ((), ())), preferred_element_type=jnp.float32)


def nn(a, b):
    return jnp.dot(a, b, preferred_element_type=jnp.float32)


def split_kernel(
    ids_ref,
    home_ref,
    keys_ref,
    values_ref,
    out_ref,
    inside,
    parts,
    ids,
    home,
    in_sems,
    out_sems,
    list_sems,
):
    blocks, tokens, width = keys_ref.shape
    groups = tokens // SLICE
    arrive = []
    for t in range(groups):
        for kind, src in enumerate((keys_ref, values_ref)):
            copy = pltpu.make_async_copy(
                src.at[:, pl.ds(t * SLICE, SLICE)], inside.at[t, kind], in_sems.at[t, kind]
            )
            copy.start()
            arrive.append(copy)
    lists = ((ids_ref, ids), (home_ref, home))
    lists = [
        pltpu.make_async_copy(src, dst, list_sems.at[n]) for n, (src, dst) in enumerate(lists)
    ]
    for copy in lists:
        copy.start()
    for copy in lists:
        copy.wait()
    line = lax.broadcasted_iota(jnp.int32, (SLICE, HD), 0)
    lane = lax.broadcasted_iota(jnp.int32, (SLICE, HD), 1)
    tag = jnp.zeros((SLICE, HD), jnp.int32)
    for k in range(ids.shape[1]):
        storage = home[ids[0, k]]
        owner = lax.div(storage, blocks)
        tag = jnp.where((line == 0) & (lane == k), owner, tag)
        tag = jnp.where((line == 1) & (lane == k), storage - owner * blocks, tag)
    tag = tag.astype(jnp.float32).astype(jnp.bfloat16)
    leave = []
    for t in range(groups):
        for kind in range(KINDS):
            arrive[t * KINDS + kind].wait()
        for part in range(HEADS * KINDS):
            m = t * HEADS * KINDS + part
            h, kind = part // KINDS, part % KINDS
            parts[m, pl.ds(0, blocks)] = inside[t, kind, :, :, h * HD : (h + 1) * HD]
            parts[m, blocks] = tag
            copy = pltpu.make_async_copy(parts.at[m], out_ref.at[m], out_sems.at[m])
            copy.start()
            leave.append(copy)
    for copy in leave:
        copy.wait()


def split(block_ids, block_home, cart_keys, cart_values, count):
    blocks, tokens, width = cart_keys.shape
    groups = tokens // SLICE
    hbm = pl.BlockSpec(memory_space=pltpu.HBM)
    return pl.pallas_call(
        split_kernel,
        out_shape=jax.ShapeDtypeStruct((count, blocks + 1, SLICE, HD), jnp.bfloat16),
        in_specs=[hbm] * 4,
        out_specs=hbm,
        scratch_shapes=[
            pltpu.VMEM((groups, KINDS, blocks, SLICE, width), jnp.bfloat16),
            pltpu.VMEM((count, blocks + 1, SLICE, HD), jnp.bfloat16),
            pltpu.SMEM(block_ids.shape, jnp.int32),
            pltpu.SMEM(block_home.shape, jnp.int32),
            pltpu.SemaphoreType.DMA((groups, KINDS)),
            pltpu.SemaphoreType.DMA((count,)),
            pltpu.SemaphoreType.DMA((2,)),
        ],
        name="split_blocks",
    )(block_ids, block_home, cart_keys, cart_values)


def pick_kernel(index_ref, length_ref, held_ref, out_ref, used_ref):
    used_ref[...] = jnp.full(used_ref.shape, length_ref[0], jnp.int32)

    def step(n, carry):
        for u in range(16):
            out_ref[n * 16 + u] = held_ref[index_ref[n * 16 + u]]
        return carry

    lax.fori_loop(0, out_ref.shape[0] // 16, step, 0)


def pick(index, length, held):
    smem = pl.BlockSpec(memory_space=pltpu.SMEM)
    vmem = pl.BlockSpec(memory_space=pltpu.VMEM)
    return pl.pallas_call(
        pick_kernel,
        out_shape=(
            jax.ShapeDtypeStruct((index.shape[0],) + held.shape[1:], jnp.bfloat16),
            jax.ShapeDtypeStruct((8, HD), jnp.int32),
        ),
        in_specs=[smem, smem, vmem],
        out_specs=(vmem, vmem),
        compiler_params=pltpu.CompilerParams(vmem_limit_bytes=16 * MIB),
        name="pick_requested",
    )(index, length, held)


def attend_kernel(
    length_ref,
    kv_ref,
    q_ref,
    g_ref,
    own_k_ref,
    own_v_ref,
    send_ref,
    out_ref,
    slope_ref,
    own_slope_ref,
    score,
    expo,
    acc,
    q_rows,
    g_cols,
):
    used = length_ref[0:1, 0:1]
    chunks = kv_ref.shape[0] // (HEADS * KINDS)
    chunk = kv_ref.shape[1]
    rows = q_rows.shape[0]
    queries = q_ref.shape[0]
    repeat = rows // queries
    own = own_k_ref.shape[0]
    scale = 1.0 / math.sqrt(HD)
    log2e = scale * math.log2(math.e)
    position = lax.rem(lax.broadcasted_iota(jnp.int32, (1, rows), 1), queries)
    row_used = position < used
    own_at = lax.broadcasted_iota(jnp.int32, (own, rows), 0)
    seen = (own_at <= position) & (own_at < used)
    for head in range(HEADS):
        lanes = slice(head * HD, (head + 1) * HD)
        own_k = own_k_ref[:, lanes]
        own_v = own_v_ref[:, lanes]
        at = lambda c, kind: (c * HEADS + head) * KINDS + kind
        for r in range(repeat):
            cols = slice((head * repeat + r) * HD, (head * repeat + r + 1) * HD)
            q_rows[r * queries : (r + 1) * queries] = q_ref[:, cols]
            g_cols[:, r * queries : (r + 1) * queries] = g_ref[:, cols].T
        own_s = jnp.where(seen, nt(own_k, q_rows[...]), -1e30)
        top = jnp.max(own_s.reshape(own // 8, 8, rows), axis=0)
        for c in range(chunks):
            s = nt(kv_ref[at(c, 0)], q_rows[...])
            score[c] = s
            top = jnp.maximum(top, jnp.max(s.reshape(chunk // 8, 8, rows), axis=0))
        top = jnp.max(top, axis=0, keepdims=True) * log2e
        e = jnp.exp2(own_s * log2e - top)
        total = jnp.sum(e.reshape(own // 8, 8, rows), axis=0)
        own_e = e.astype(jnp.bfloat16)
        acc[...] = nn(own_v.T, own_e)
        for c in range(chunks):
            e = jnp.exp2(score[c] * log2e - top)
            total = total + jnp.sum(e.reshape(chunk // 8, 8, rows), axis=0)
            low = e.astype(jnp.bfloat16)
            expo[c] = low
            acc[...] += nn(kv_ref[at(c, 1)].T, low)
        inv = 1.0 / jnp.sum(total, axis=0, keepdims=True)
        g = jnp.where(row_used, g_cols[...].astype(jnp.float32), 0.0)
        out = jnp.where(row_used, acc[...] * inv, 0.0)
        out_ref[head] = out
        delta = jnp.sum(g * out, axis=0, keepdims=True) * inv
        gs = (g * inv).astype(jnp.bfloat16)
        ds = own_e.astype(jnp.float32) * (nn(own_v, gs) - delta)
        own_slope_ref[head] = ds.astype(jnp.bfloat16)
        for c in range(chunks):
            low = expo[c]
            send_ref[at(c, 1)] = nt(low, gs).astype(jnp.bfloat16)
            dp = nn(kv_ref[at(c, 1)], gs)
            ds = (low.astype(jnp.float32) * (dp - delta)).astype(jnp.bfloat16)
            slope_ref[head, c] = ds
            send_ref[at(c, 0)] = (nn(ds, q_rows[...]) * scale).astype(jnp.bfloat16)


def attend(length, kv, q, g, own_k, own_v):
    count, chunk, _ = kv.shape
    queries, width = q.shape
    rows = queries * width // (HEADS * HD)
    chunks = count // (HEADS * KINDS)
    vmem = pl.BlockSpec(memory_space=pltpu.VMEM)
    return pl.pallas_call(
        attend_kernel,
        out_shape=(
            jax.ShapeDtypeStruct(kv.shape, jnp.bfloat16),
            jax.ShapeDtypeStruct((HEADS, HD, rows), jnp.float32),
            jax.ShapeDtypeStruct((HEADS, chunks, chunk, rows), jnp.bfloat16),
            jax.ShapeDtypeStruct((HEADS, own_k.shape[0], rows), jnp.bfloat16),
        ),
        in_specs=[vmem] * 6,
        out_specs=(vmem,) * 4,
        scratch_shapes=[
            pltpu.VMEM((chunks, chunk, rows), jnp.float32),
            pltpu.VMEM((chunks, chunk, rows), jnp.bfloat16),
            pltpu.VMEM((HD, rows), jnp.float32),
            pltpu.VMEM((rows, HD), jnp.bfloat16),
            pltpu.VMEM((HD, rows), jnp.bfloat16),
        ],
        compiler_params=pltpu.CompilerParams(vmem_limit_bytes=36 * MIB),
        cost_estimate=pl.CostEstimate(
            flops=10 * 2 * HD * rows * (chunks * chunk + queries),
            bytes_accessed=8 * MIB,
            transcendentals=HEADS * rows * chunks * chunk,
        ),
        name="attend_forward_backward",
    )(length, kv, q, g, own_k, own_v)


def rows_kernel(kv_ref, own_k_ref, out_t_ref, slope_ref, own_slope_ref, out_ref, grad_q_ref):
    chunks = slope_ref.shape[1]
    rows = out_t_ref.shape[2]
    queries = out_ref.shape[0]
    repeat = rows // queries
    scale = 1.0 / math.sqrt(HD)
    for head in range(HEADS):
        own_k = own_k_ref[:, head * HD : (head + 1) * HD]
        grad = nn(own_k.T, own_slope_ref[head])
        for c in range(chunks):
            grad += nn(kv_ref[(c * HEADS + head) * KINDS].T, slope_ref[head, c])
        grad = grad * scale
        out = out_t_ref[head]
        for r in range(repeat):
            cols = slice((head * repeat + r) * HD, (head * repeat + r + 1) * HD)
            at = slice(r * queries, (r + 1) * queries)
            out_ref[:, cols] = out[:, at].T.astype(jnp.bfloat16)
            grad_q_ref[:, cols] = grad[:, at].T.astype(jnp.bfloat16)


def query_rows(kv, own_k, out_t, slope, own_slope, queries, width):
    vmem = pl.BlockSpec(memory_space=pltpu.VMEM)
    shape = jax.ShapeDtypeStruct((queries, width), jnp.bfloat16)
    return pl.pallas_call(
        rows_kernel,
        out_shape=(shape, shape),
        in_specs=[vmem] * 5,
        out_specs=(vmem, vmem),
        compiler_params=pltpu.CompilerParams(vmem_limit_bytes=24 * MIB),
        cost_estimate=pl.CostEstimate(
            flops=2 * HD * HEADS * out_t.shape[2] * kv.shape[0] * kv.shape[1] // 2,
            bytes_accessed=12 * MIB,
            transcendentals=0,
        ),
        name="outputs_by_query",
    )(kv, own_k, out_t, slope, own_slope)


def add_kernel(index_ref, got_ref, out_ref, table):
    selected = index_ref.shape[1]
    owners, held = out_ref.shape[0], out_ref.shape[1] - TAG
    blocks = held // SLICE
    table[...] = jnp.zeros_like(table)

    def step(n, carry):
        at = [index_ref[n, k] for k in range(selected)]
        sums = [table[at[k]] + got_ref[n, k].astype(jnp.float32) for k in range(selected)]
        for k in range(selected):
            table[at[k]] = sums[k]
        return carry

    lax.fori_loop(0, got_ref.shape[0], step, 0, unroll=4)

    def finish(n, squares):
        rows = table[pl.ds(n * blocks, blocks)].reshape(held, HD)
        out_ref[n, pl.ds(0, held)] = rows.astype(jnp.bfloat16)
        return squares + jnp.sum((rows * rows).reshape(held // 8, 8, HD), axis=0)

    squares = lax.fori_loop(0, owners, finish, jnp.zeros((8, HD), jnp.float32), unroll=4)
    squares = squares[: TAG // 2] + squares[TAG // 2 :]
    high = squares.astype(jnp.bfloat16).astype(jnp.float32)
    tag = jnp.concatenate([high, squares - high], axis=0).astype(jnp.bfloat16)
    for n in range(owners):
        out_ref[n, pl.ds(held, TAG)] = tag


def add_up(index, got, blk_dev):
    count = got.shape[0]
    vmem = pl.BlockSpec(memory_space=pltpu.VMEM)
    return pl.pallas_call(
        add_kernel,
        out_shape=jax.ShapeDtypeStruct((count, blk_dev * SLICE + TAG, HD), jnp.bfloat16),
        in_specs=[pl.BlockSpec(memory_space=pltpu.SMEM), vmem],
        out_specs=vmem,
        scratch_shapes=[pltpu.VMEM((count * blk_dev, SLICE, HD), jnp.float32)],
        compiler_params=pltpu.CompilerParams(vmem_limit_bytes=24 * MIB),
        name="add_over_readers",
    )(index, got)


def finish_kernel(count, *refs):
    squares, (got_ref, key_ref, value_ref, keys, values, sems) = refs[:-6], refs[-6:]
    total = jnp.sum(sum(ref[...] for ref in squares), axis=(0, 1), keepdims=True)
    inv = 1.0 / jnp.sqrt(total / count + 1e-6)
    parts = sems.shape[0]
    step = keys.shape[0] // parts
    copies = []
    for n in range(parts):
        at = pl.ds(n * step, step)
        for m in range(got_ref.shape[0]):
            t, h, kind = m // 4, (m // 2) % 2, m % 2
            part = got_ref[m, n * step * SLICE : (n + 1) * step * SLICE].astype(jnp.float32) * inv
            part = part.reshape(step, SLICE, HD)
            (keys, values)[kind][at, t * SLICE : (t + 1) * SLICE, h * HD : (h + 1) * HD] = part
        for kind, (src, dst) in enumerate(((keys, key_ref), (values, value_ref))):
            copies.append(pltpu.make_async_copy(src.at[at], dst.at[at], sems.at[n, kind]))
            copies[-1].start()
    for copy in copies:
        copy.wait()


def finish(squares, got, block_tok, width, count):
    blocks = (got.shape[1] - TAG) // SLICE
    vmem = pl.BlockSpec(memory_space=pltpu.VMEM)
    hbm = pl.BlockSpec(memory_space=pltpu.HBM)
    shape = (blocks, block_tok, width)
    return pl.pallas_call(
        functools.partial(finish_kernel, count),
        out_shape=(jax.ShapeDtypeStruct(shape, jnp.float32),) * 2,
        in_specs=[vmem] * (len(squares) + 1),
        out_specs=(hbm, hbm),
        scratch_shapes=[
            pltpu.VMEM(shape, jnp.float32),
            pltpu.VMEM(shape, jnp.float32),
            pltpu.SemaphoreType.DMA((4, KINDS)),
        ],
        compiler_params=pltpu.CompilerParams(vmem_limit_bytes=24 * MIB),
        name="normalize_updates",
    )(*squares, got)


def swap(a):
    return lax.all_to_all(a, "wide", split_axis=0, concat_axis=0, tiled=True)


def local(
    queries,
    own_keys,
    own_values,
    cart_keys,
    cart_values,
    block_ids,
    block_home,
    query_len,
    grad_out,
):
    wide_count = lax.axis_size("wide")
    blk_dev, block_tok, width = cart_keys.shape
    selected = block_ids.shape[1]
    all_blocks = block_home.shape[0]
    held = swap(split(block_ids, block_home, cart_keys, cart_values, wide_count))
    asked = held[:, blk_dev, :2, :selected].astype(jnp.int32)
    owner, row = asked[:, 0], asked[:, 1]
    picked, used = pick(
        (owner * (blk_dev + 1) + row).reshape(-1),
        query_len,
        held.reshape(wide_count * (blk_dev + 1), SLICE, HD),
    )
    kv = swap(picked.reshape(wide_count, selected * SLICE, HD))
    send, out_t, slope, own_slope = attend(
        used, kv, queries[0], grad_out[0], own_keys[0], own_values[0]
    )
    got = swap(send).reshape(wide_count, selected, SLICE, HD)
    back = swap(add_up(owner * blk_dev + row, got, blk_dev))
    squares = jnp.sum(back[:, -TAG:].astype(jnp.float32), axis=0)
    mp = lax.axis_size("mp")
    shifts = [[(i, (i + d) % mp) for i in range(mp)] for d in range(1, mp)]
    squares = [squares] + [lax.ppermute(squares, "mp", pairs) for pairs in shifts]
    out_t, slope, _ = lax.optimization_barrier((out_t, slope, back))
    attn_out, grad_queries = query_rows(
        kv, own_keys[0], out_t, slope, own_slope, queries.shape[1], queries.shape[2]
    )
    count = 2.0 * all_blocks * block_tok * width * mp
    key_update, value_update = finish(squares, back, block_tok, width, count)
    return (attn_out[None], grad_queries[None], key_update, value_update)


def solution(mesh):
    shared = P("wide", None, "mp")
    return jax.shard_map(
        local,
        mesh=mesh,
        in_specs=(shared, shared, shared, shared, shared, P("wide", None), P(), P("wide"), shared),
        out_specs=(shared, shared, shared, shared),
        check_vma=False,
    )
```

```python
import functools
import math

import jax
import jax.numpy as jnp
from jax import lax
from jax.experimental import pallas as pl
from jax.experimental.pallas import tpu as pltpu
from jax.sharding import PartitionSpec as P

HD = 128
SLICE = 16
TAG = 16
HEADS = 2
KINDS = 2
MIB = 1024 * 1024


def nt(a, b):
    return lax.dot_general(a, b, (((1,), (1,)), ((), ())), preferred_element_type=jnp.float32)


def nn(a, b):
    return jnp.dot(a, b, preferred_element_type=jnp.float32)


def split_kernel(
    ids_ref,
    home_ref,
    keys_ref,
    values_ref,
    out_ref,
    inside,
    parts,
    ids,
    home,
    in_sems,
    out_sems,
    list_sems,
):
    blocks, tokens, width = keys_ref.shape
    groups = tokens // SLICE
    arrive = []
    for t in range(groups):
        for kind, src in enumerate((keys_ref, values_ref)):
            copy = pltpu.make_async_copy(
                src.at[:, pl.ds(t * SLICE, SLICE)], inside.at[t, kind], in_sems.at[t, kind]
            )
            copy.start()
            arrive.append(copy)
    lists = ((ids_ref, ids), (home_ref, home))
    lists = [
        pltpu.make_async_copy(src, dst, list_sems.at[n]) for n, (src, dst) in enumerate(lists)
    ]
    for copy in lists:
        copy.start()
    for copy in lists:
        copy.wait()
    line = lax.broadcasted_iota(jnp.int32, (SLICE, HD), 0)
    lane = lax.broadcasted_iota(jnp.int32, (SLICE, HD), 1)
    tag = jnp.zeros((SLICE, HD), jnp.int32)
    for k in range(ids.shape[1]):
        storage = home[ids[0, k]]
        owner = lax.div(storage, blocks)
        tag = jnp.where((line == 0) & (lane == k), owner, tag)
        tag = jnp.where((line == 1) & (lane == k), storage - owner * blocks, tag)
    tag = tag.astype(jnp.float32).astype(jnp.bfloat16)
    leave = []
    for t in range(groups):
        for kind in range(KINDS):
            arrive[t * KINDS + kind].wait()
        for part in range(HEADS * KINDS):
            m = t * HEADS * KINDS + part
            h, kind = part // KINDS, part % KINDS
            parts[m, pl.ds(0, blocks)] = inside[t, kind, :, :, h * HD : (h + 1) * HD]
            parts[m, blocks] = tag
            copy = pltpu.make_async_copy(parts.at[m], out_ref.at[m], out_sems.at[m])
            copy.start()
            leave.append(copy)
    for copy in leave:
        copy.wait()


def split(block_ids, block_home, cart_keys, cart_values, count):
    blocks, tokens, width = cart_keys.shape
    groups = tokens // SLICE
    hbm = pl.BlockSpec(memory_space=pltpu.HBM)
    return pl.pallas_call(
        split_kernel,
        out_shape=jax.ShapeDtypeStruct((count, blocks + 1, SLICE, HD), jnp.bfloat16),
        in_specs=[hbm] * 4,
        out_specs=hbm,
        scratch_shapes=[
            pltpu.VMEM((groups, KINDS, blocks, SLICE, width), jnp.bfloat16),
            pltpu.VMEM((count, blocks + 1, SLICE, HD), jnp.bfloat16),
            pltpu.SMEM(block_ids.shape, jnp.int32),
            pltpu.SMEM(block_home.shape, jnp.int32),
            pltpu.SemaphoreType.DMA((groups, KINDS)),
            pltpu.SemaphoreType.DMA((count,)),
            pltpu.SemaphoreType.DMA((2,)),
        ],
        name="split_blocks",
    )(block_ids, block_home, cart_keys, cart_values)


def pick_kernel(index_ref, length_ref, held_ref, out_ref, used_ref):
    used_ref[...] = jnp.full(used_ref.shape, length_ref[0], jnp.int32)

    def step(n, carry):
        for u in range(16):
            out_ref[n * 16 + u] = held_ref[index_ref[n * 16 + u]]
        return carry

    lax.fori_loop(0, out_ref.shape[0] // 16, step, 0, unroll=2)


def pick(index, length, held):
    smem = pl.BlockSpec(memory_space=pltpu.SMEM)
    vmem = pl.BlockSpec(memory_space=pltpu.VMEM)
    return pl.pallas_call(
        pick_kernel,
        out_shape=(
            jax.ShapeDtypeStruct((index.shape[0],) + held.shape[1:], jnp.bfloat16),
            jax.ShapeDtypeStruct((8, HD), jnp.int32),
        ),
        in_specs=[smem, smem, vmem],
        out_specs=(vmem, vmem),
        compiler_params=pltpu.CompilerParams(vmem_limit_bytes=16 * MIB),
        name="pick_requested",
    )(index, length, held)


def attend_kernel(
    length_ref,
    kv_ref,
    q_ref,
    g_ref,
    own_k_ref,
    own_v_ref,
    send_ref,
    out_ref,
    slope_ref,
    own_slope_ref,
    score,
    expo,
    acc,
    q_rows,
    g_cols,
):
    used = length_ref[0:1, 0:1]
    chunks = kv_ref.shape[0] // (HEADS * KINDS)
    chunk = kv_ref.shape[1]
    rows = q_rows.shape[0]
    queries = q_ref.shape[0]
    repeat = rows // queries
    own = own_k_ref.shape[0]
    scale = 1.0 / math.sqrt(HD)
    log2e = scale * math.log2(math.e)
    position = lax.rem(lax.broadcasted_iota(jnp.int32, (1, rows), 1), queries)
    row_used = position < used
    own_at = lax.broadcasted_iota(jnp.int32, (own, rows), 0)
    seen = (own_at <= position) & (own_at < used)
    for head in range(HEADS):
        lanes = slice(head * HD, (head + 1) * HD)
        own_k = own_k_ref[:, lanes]
        own_v = own_v_ref[:, lanes]
        at = lambda c, kind: (c * HEADS + head) * KINDS + kind
        for r in range(repeat):
            cols = slice((head * repeat + r) * HD, (head * repeat + r + 1) * HD)
            q_rows[r * queries : (r + 1) * queries] = q_ref[:, cols]
            g_cols[:, r * queries : (r + 1) * queries] = g_ref[:, cols].T
        own_s = jnp.where(seen, nt(own_k, q_rows[...]), -1e30)
        top = jnp.max(own_s.reshape(own // 8, 8, rows), axis=0)
        for c in range(chunks):
            s = nt(kv_ref[at(c, 0)], q_rows[...])
            score[c] = s
            top = jnp.maximum(top, jnp.max(s.reshape(chunk // 8, 8, rows), axis=0))
        top = jnp.max(top, axis=0, keepdims=True) * log2e
        e = jnp.exp2(own_s * log2e - top)
        total = jnp.sum(e.reshape(own // 8, 8, rows), axis=0)
        own_e = e.astype(jnp.bfloat16)
        acc[...] = nn(own_v.T, own_e)
        for c in range(chunks):
            e = jnp.exp2(score[c] * log2e - top)
            total = total + jnp.sum(e.reshape(chunk // 8, 8, rows), axis=0)
            low = e.astype(jnp.bfloat16)
            expo[c] = low
            acc[...] += nn(kv_ref[at(c, 1)].T, low)
        inv = 1.0 / jnp.sum(total, axis=0, keepdims=True)
        g = jnp.where(row_used, g_cols[...].astype(jnp.float32), 0.0)
        out = jnp.where(row_used, acc[...] * inv, 0.0)
        out_ref[head] = out
        delta = jnp.sum(g * out, axis=0, keepdims=True) * inv
        gs = (g * inv).astype(jnp.bfloat16)
        ds = own_e.astype(jnp.float32) * (nn(own_v, gs) - delta)
        own_slope_ref[head] = ds.astype(jnp.bfloat16)
        for c in range(chunks):
            low = expo[c]
            send_ref[at(c, 1)] = nt(low, gs).astype(jnp.bfloat16)
            dp = nn(kv_ref[at(c, 1)], gs)
            ds = (low.astype(jnp.float32) * (dp - delta)).astype(jnp.bfloat16)
            slope_ref[head, c] = ds
            send_ref[at(c, 0)] = (nn(ds, q_rows[...]) * scale).astype(jnp.bfloat16)


def attend(length, kv, q, g, own_k, own_v):
    count, chunk, _ = kv.shape
    queries, width = q.shape
    rows = queries * width // (HEADS * HD)
    chunks = count // (HEADS * KINDS)
    vmem = pl.BlockSpec(memory_space=pltpu.VMEM)
    return pl.pallas_call(
        attend_kernel,
        out_shape=(
            jax.ShapeDtypeStruct(kv.shape, jnp.bfloat16),
            jax.ShapeDtypeStruct((HEADS, HD, rows), jnp.float32),
            jax.ShapeDtypeStruct((HEADS, chunks, chunk, rows), jnp.bfloat16),
            jax.ShapeDtypeStruct((HEADS, own_k.shape[0], rows), jnp.bfloat16),
        ),
        in_specs=[vmem] * 6,
        out_specs=(vmem,) * 4,
        scratch_shapes=[
            pltpu.VMEM((chunks, chunk, rows), jnp.float32),
            pltpu.VMEM((chunks, chunk, rows), jnp.bfloat16),
            pltpu.VMEM((HD, rows), jnp.float32),
            pltpu.VMEM((rows, HD), jnp.bfloat16),
            pltpu.VMEM((HD, rows), jnp.bfloat16),
        ],
        compiler_params=pltpu.CompilerParams(vmem_limit_bytes=36 * MIB),
        cost_estimate=pl.CostEstimate(
            flops=10 * 2 * HD * rows * (chunks * chunk + queries),
            bytes_accessed=8 * MIB,
            transcendentals=HEADS * rows * chunks * chunk,
        ),
        name="attend_forward_backward",
    )(length, kv, q, g, own_k, own_v)


def rows_kernel(kv_ref, own_k_ref, out_t_ref, slope_ref, own_slope_ref, out_ref, grad_q_ref):
    chunks = slope_ref.shape[1]
    rows = out_t_ref.shape[2]
    queries = out_ref.shape[0]
    repeat = rows // queries
    scale = 1.0 / math.sqrt(HD)
    for head in range(HEADS):
        own_k = own_k_ref[:, head * HD : (head + 1) * HD]
        grad = nn(own_k.T, own_slope_ref[head])
        for c in range(chunks):
            grad += nn(kv_ref[(c * HEADS + head) * KINDS].T, slope_ref[head, c])
        grad = grad * scale
        out = out_t_ref[head]
        for r in range(repeat):
            cols = slice((head * repeat + r) * HD, (head * repeat + r + 1) * HD)
            at = slice(r * queries, (r + 1) * queries)
            out_ref[:, cols] = out[:, at].T.astype(jnp.bfloat16)
            grad_q_ref[:, cols] = grad[:, at].T.astype(jnp.bfloat16)


def query_rows(kv, own_k, out_t, slope, own_slope, queries, width):
    vmem = pl.BlockSpec(memory_space=pltpu.VMEM)
    shape = jax.ShapeDtypeStruct((queries, width), jnp.bfloat16)
    return pl.pallas_call(
        rows_kernel,
        out_shape=(shape, shape),
        in_specs=[vmem] * 5,
        out_specs=(vmem, vmem),
        compiler_params=pltpu.CompilerParams(vmem_limit_bytes=24 * MIB),
        cost_estimate=pl.CostEstimate(
            flops=2 * HD * HEADS * out_t.shape[2] * kv.shape[0] * kv.shape[1] // 2,
            bytes_accessed=12 * MIB,
            transcendentals=0,
        ),
        name="outputs_by_query",
    )(kv, own_k, out_t, slope, own_slope)


def add_kernel(index_ref, got_ref, out_ref, table):
    selected = index_ref.shape[1]
    owners, held = out_ref.shape[0], out_ref.shape[1] - TAG
    blocks = held // SLICE
    table[...] = jnp.zeros_like(table)

    def step(n, carry):
        at = [index_ref[n, k] for k in range(selected)]
        sums = [table[at[k]] + got_ref[n, k].astype(jnp.float32) for k in range(selected)]
        for k in range(selected):
            table[at[k]] = sums[k]
        return carry

    lax.fori_loop(0, got_ref.shape[0], step, 0, unroll=4)

    def finish(n, squares):
        rows = table[pl.ds(n * blocks, blocks)].reshape(held, HD)
        out_ref[n, pl.ds(0, held)] = rows.astype(jnp.bfloat16)
        return squares + jnp.sum((rows * rows).reshape(held // 8, 8, HD), axis=0)

    squares = lax.fori_loop(0, owners, finish, jnp.zeros((8, HD), jnp.float32), unroll=4)
    high = squares.astype(jnp.bfloat16).astype(jnp.float32)
    tag = jnp.concatenate([high, squares - high], axis=0).astype(jnp.bfloat16)
    for n in range(owners):
        out_ref[n, pl.ds(held, TAG)] = tag


def add_up(index, got, blk_dev):
    count = got.shape[0]
    vmem = pl.BlockSpec(memory_space=pltpu.VMEM)
    return pl.pallas_call(
        add_kernel,
        out_shape=jax.ShapeDtypeStruct((count, blk_dev * SLICE + TAG, HD), jnp.bfloat16),
        in_specs=[pl.BlockSpec(memory_space=pltpu.SMEM), vmem],
        out_specs=vmem,
        scratch_shapes=[pltpu.VMEM((count * blk_dev, SLICE, HD), jnp.float32)],
        compiler_params=pltpu.CompilerParams(vmem_limit_bytes=24 * MIB),
        name="add_over_readers",
    )(index, got)


def finish_kernel(count, *refs):
    squares, (got_ref, key_ref, value_ref, keys, values, sems) = refs[:-6], refs[-6:]
    total = jnp.sum(sum(ref[...] for ref in squares), axis=(0, 1), keepdims=True)
    inv = 1.0 / jnp.sqrt(total / count + 1e-6)
    parts = sems.shape[0]
    step = keys.shape[0] // parts
    copies = []
    for n in range(parts):
        at = pl.ds(n * step, step)
        for m in range(got_ref.shape[0]):
            t, h, kind = m // 4, (m // 2) % 2, m % 2
            part = got_ref[m, n * step * SLICE : (n + 1) * step * SLICE].astype(jnp.float32) * inv
            part = part.reshape(step, SLICE, HD)
            (keys, values)[kind][at, t * SLICE : (t + 1) * SLICE, h * HD : (h + 1) * HD] = part
        for kind, (src, dst) in enumerate(((keys, key_ref), (values, value_ref))):
            copies.append(pltpu.make_async_copy(src.at[at], dst.at[at], sems.at[n, kind]))
            copies[-1].start()
    for copy in copies:
        copy.wait()


def finish(squares, got, block_tok, width, count):
    blocks = (got.shape[1] - TAG) // SLICE
    vmem = pl.BlockSpec(memory_space=pltpu.VMEM)
    hbm = pl.BlockSpec(memory_space=pltpu.HBM)
    shape = (blocks, block_tok, width)
    return pl.pallas_call(
        functools.partial(finish_kernel, count),
        out_shape=(jax.ShapeDtypeStruct(shape, jnp.float32),) * 2,
        in_specs=[vmem] * (len(squares) + 1),
        out_specs=(hbm, hbm),
        scratch_shapes=[
            pltpu.VMEM(shape, jnp.float32),
            pltpu.VMEM(shape, jnp.float32),
            pltpu.SemaphoreType.DMA((4, KINDS)),
        ],
        compiler_params=pltpu.CompilerParams(vmem_limit_bytes=24 * MIB),
        name="normalize_updates",
    )(*squares, got)


def swap(a):
    return lax.all_to_all(a, "wide", split_axis=0, concat_axis=0, tiled=True)


def local(
    queries,
    own_keys,
    own_values,
    cart_keys,
    cart_values,
    block_ids,
    block_home,
    query_len,
    grad_out,
):
    wide_count = lax.axis_size("wide")
    blk_dev, block_tok, width = cart_keys.shape
    selected = block_ids.shape[1]
    all_blocks = block_home.shape[0]
    held = swap(split(block_ids, block_home, cart_keys, cart_values, wide_count))
    asked = held[:, blk_dev, :2, :selected].astype(jnp.int32)
    owner, row = asked[:, 0], asked[:, 1]
    picked, used = pick(
        (owner * (blk_dev + 1) + row).reshape(-1),
        query_len,
        held.reshape(wide_count * (blk_dev + 1), SLICE, HD),
    )
    kv = swap(picked.reshape(wide_count, selected * SLICE, HD))
    send, out_t, slope, own_slope = attend(
        used, kv, queries[0], grad_out[0], own_keys[0], own_values[0]
    )
    got = swap(send).reshape(wide_count, selected, SLICE, HD)
    back = swap(add_up(owner * blk_dev + row, got, blk_dev))
    squares = back[:, -TAG:].astype(jnp.float32).reshape(2 * wide_count, TAG // 2, HD)
    squares = jnp.sum(squares, axis=0)
    mp = lax.axis_size("mp")
    shifts = [[(i, (i + d) % mp) for i in range(mp)] for d in range(1, mp)]
    squares = [squares] + [lax.ppermute(squares, "mp", pairs) for pairs in shifts]
    out_t, slope, _ = lax.optimization_barrier((out_t, slope, back))
    attn_out, grad_queries = query_rows(
        kv, own_keys[0], out_t, slope, own_slope, queries.shape[1], queries.shape[2]
    )
    count = 2.0 * all_blocks * block_tok * width * mp
    key_update, value_update = finish(squares, back, block_tok, width, count)
    return (attn_out[None], grad_queries[None], key_update, value_update)


def solution(mesh):
    shared = P("wide", None, "mp")
    return jax.shard_map(
        local,
        mesh=mesh,
        in_specs=(shared, shared, shared, shared, shared, P("wide", None), P(), P("wide"), shared),
        out_specs=(shared, shared, shared, shared),
        check_vma=False,
    )
```

```python
import functools
import math

import jax
import jax.numpy as jnp
from jax import lax
from jax.experimental import pallas as pl
from jax.experimental.pallas import tpu as pltpu
from jax.sharding import PartitionSpec as P

HD = 128
SLICE = 16
TAG = 16
HEADS = 2
KINDS = 2
MIB = 1024 * 1024


def nt(a, b):
    return lax.dot_general(a, b, (((1,), (1,)), ((), ())), preferred_element_type=jnp.float32)


def nn(a, b):
    return jnp.dot(a, b, preferred_element_type=jnp.float32)


def split_kernel(
    ids_ref,
    home_ref,
    keys_ref,
    values_ref,
    out_ref,
    inside,
    parts,
    ids,
    home,
    in_sems,
    out_sems,
    list_sems,
):
    blocks, tokens, width = keys_ref.shape
    groups = tokens // SLICE
    arrive = []
    for t in range(groups):
        for kind, src in enumerate((keys_ref, values_ref)):
            copy = pltpu.make_async_copy(
                src.at[:, pl.ds(t * SLICE, SLICE)], inside.at[t, kind], in_sems.at[t, kind]
            )
            copy.start()
            arrive.append(copy)
    lists = ((ids_ref, ids), (home_ref, home))
    lists = [
        pltpu.make_async_copy(src, dst, list_sems.at[n]) for n, (src, dst) in enumerate(lists)
    ]
    for copy in lists:
        copy.start()
    for copy in lists:
        copy.wait()
    line = lax.broadcasted_iota(jnp.int32, (SLICE, HD), 0)
    lane = lax.broadcasted_iota(jnp.int32, (SLICE, HD), 1)
    tag = jnp.zeros((SLICE, HD), jnp.int32)
    for k in range(ids.shape[1]):
        storage = home[ids[0, k]]
        owner = lax.div(storage, blocks)
        tag = jnp.where((line == 0) & (lane == k), owner, tag)
        tag = jnp.where((line == 1) & (lane == k), storage - owner * blocks, tag)
    tag = tag.astype(jnp.float32).astype(jnp.bfloat16)
    leave = []
    for t in range(groups):
        for kind in range(KINDS):
            arrive[t * KINDS + kind].wait()
        for part in range(HEADS * KINDS):
            m = t * HEADS * KINDS + part
            h, kind = part // KINDS, part % KINDS
            parts[m, pl.ds(0, blocks)] = inside[t, kind, :, :, h * HD : (h + 1) * HD]
            parts[m, blocks] = tag
            copy = pltpu.make_async_copy(parts.at[m], out_ref.at[m], out_sems.at[m])
            copy.start()
            leave.append(copy)
    for copy in leave:
        copy.wait()


def split(block_ids, block_home, cart_keys, cart_values, count):
    blocks, tokens, width = cart_keys.shape
    groups = tokens // SLICE
    hbm = pl.BlockSpec(memory_space=pltpu.HBM)
    return pl.pallas_call(
        split_kernel,
        out_shape=jax.ShapeDtypeStruct((count, blocks + 1, SLICE, HD), jnp.bfloat16),
        in_specs=[hbm] * 4,
        out_specs=hbm,
        scratch_shapes=[
            pltpu.VMEM((groups, KINDS, blocks, SLICE, width), jnp.bfloat16),
            pltpu.VMEM((count, blocks + 1, SLICE, HD), jnp.bfloat16),
            pltpu.SMEM(block_ids.shape, jnp.int32),
            pltpu.SMEM(block_home.shape, jnp.int32),
            pltpu.SemaphoreType.DMA((groups, KINDS)),
            pltpu.SemaphoreType.DMA((count,)),
            pltpu.SemaphoreType.DMA((2,)),
        ],
        name="split_blocks",
    )(block_ids, block_home, cart_keys, cart_values)


def pick_kernel(index_ref, length_ref, held_ref, out_ref, used_ref):
    used_ref[...] = jnp.full(used_ref.shape, length_ref[0], jnp.int32)

    def step(n, carry):
        for u in range(16):
            out_ref[n * 16 + u] = held_ref[index_ref[n * 16 + u]]
        return carry

    lax.fori_loop(0, out_ref.shape[0] // 16, step, 0, unroll=2)


def pick(index, length, held):
    smem = pl.BlockSpec(memory_space=pltpu.SMEM)
    vmem = pl.BlockSpec(memory_space=pltpu.VMEM)
    return pl.pallas_call(
        pick_kernel,
        out_shape=(
            jax.ShapeDtypeStruct((index.shape[0],) + held.shape[1:], jnp.bfloat16),
            jax.ShapeDtypeStruct((8, HD), jnp.int32),
        ),
        in_specs=[smem, smem, vmem],
        out_specs=(vmem, vmem),
        compiler_params=pltpu.CompilerParams(vmem_limit_bytes=16 * MIB),
        name="pick_requested",
    )(index, length, held)


def attend_kernel(
    length_ref,
    kv_ref,
    q_ref,
    g_ref,
    own_k_ref,
    own_v_ref,
    send_ref,
    out_ref,
    slope_ref,
    own_slope_ref,
    score,
    expo,
    acc,
    q_rows,
    g_cols,
):
    used = length_ref[0:1, 0:1]
    chunks = kv_ref.shape[0] // (HEADS * KINDS)
    chunk = kv_ref.shape[1]
    rows = q_rows.shape[0]
    queries = q_ref.shape[0]
    repeat = rows // queries
    own = own_k_ref.shape[0]
    scale = 1.0 / math.sqrt(HD)
    log2e = scale * math.log2(math.e)
    position = lax.rem(lax.broadcasted_iota(jnp.int32, (1, rows), 1), queries)
    row_used = position < used
    own_at = lax.broadcasted_iota(jnp.int32, (own, rows), 0)
    seen = (own_at <= position) & (own_at < used)
    ones = jnp.ones((16, chunk), jnp.bfloat16)
    for head in range(HEADS):
        lanes = slice(head * HD, (head + 1) * HD)
        own_k = own_k_ref[:, lanes]
        own_v = own_v_ref[:, lanes]
        at = lambda c, kind: (c * HEADS + head) * KINDS + kind
        for r in range(repeat):
            cols = slice((head * repeat + r) * HD, (head * repeat + r + 1) * HD)
            q_rows[r * queries : (r + 1) * queries] = q_ref[:, cols]
            g_cols[:, r * queries : (r + 1) * queries] = g_ref[:, cols].T
        own_s = jnp.where(seen, nt(own_k, q_rows[...]), -1e30)
        top = jnp.max(own_s.reshape(own // 8, 8, rows), axis=0)
        for c in range(chunks):
            s = nt(kv_ref[at(c, 0)], q_rows[...])
            score[c] = s
            top = jnp.maximum(top, jnp.max(s.reshape(chunk // 8, 8, rows), axis=0))
        top = jnp.max(top, axis=0, keepdims=True) * log2e
        e = jnp.exp2(own_s * log2e - top)
        own_e = e.astype(jnp.bfloat16)
        acc[...] = nn(jnp.concatenate([own_v.T, ones[:, :own]], axis=0), own_e)
        for c in range(chunks):
            e = jnp.exp2(score[c] * log2e - top)
            low = e.astype(jnp.bfloat16)
            expo[c] = low
            acc[...] += nn(jnp.concatenate([kv_ref[at(c, 1)].T, ones], axis=0), low)
        inv = 1.0 / acc[HD : HD + 1]
        g = jnp.where(row_used, g_cols[...].astype(jnp.float32), 0.0)
        out = jnp.where(row_used, acc[:HD] * inv, 0.0)
        out_ref[head] = out
        delta = jnp.sum(g * out, axis=0, keepdims=True) * inv
        gs = (g * inv).astype(jnp.bfloat16)
        ds = own_e.astype(jnp.float32) * (nn(own_v, gs) - delta)
        own_slope_ref[head] = ds.astype(jnp.bfloat16)
        for c in range(chunks):
            low = expo[c]
            send_ref[at(c, 1)] = nt(low, gs).astype(jnp.bfloat16)
            dp = nn(kv_ref[at(c, 1)], gs)
            ds = (low.astype(jnp.float32) * (dp - delta)).astype(jnp.bfloat16)
            slope_ref[head, c] = ds
            send_ref[at(c, 0)] = (nn(ds, q_rows[...]) * scale).astype(jnp.bfloat16)


def attend(length, kv, q, g, own_k, own_v):
    count, chunk, _ = kv.shape
    queries, width = q.shape
    rows = queries * width // (HEADS * HD)
    chunks = count // (HEADS * KINDS)
    vmem = pl.BlockSpec(memory_space=pltpu.VMEM)
    return pl.pallas_call(
        attend_kernel,
        out_shape=(
            jax.ShapeDtypeStruct(kv.shape, jnp.bfloat16),
            jax.ShapeDtypeStruct((HEADS, HD, rows), jnp.float32),
            jax.ShapeDtypeStruct((HEADS, chunks, chunk, rows), jnp.bfloat16),
            jax.ShapeDtypeStruct((HEADS, own_k.shape[0], rows), jnp.bfloat16),
        ),
        in_specs=[vmem] * 6,
        out_specs=(vmem,) * 4,
        scratch_shapes=[
            pltpu.VMEM((chunks, chunk, rows), jnp.float32),
            pltpu.VMEM((chunks, chunk, rows), jnp.bfloat16),
            pltpu.VMEM((HD + 16, rows), jnp.float32),
            pltpu.VMEM((rows, HD), jnp.bfloat16),
            pltpu.VMEM((HD, rows), jnp.bfloat16),
        ],
        compiler_params=pltpu.CompilerParams(vmem_limit_bytes=36 * MIB),
        cost_estimate=pl.CostEstimate(
            flops=10 * 2 * HD * rows * (chunks * chunk + queries),
            bytes_accessed=8 * MIB,
            transcendentals=HEADS * rows * chunks * chunk,
        ),
        name="attend_forward_backward",
    )(length, kv, q, g, own_k, own_v)


def rows_kernel(kv_ref, own_k_ref, out_t_ref, slope_ref, own_slope_ref, out_ref, grad_q_ref):
    chunks = slope_ref.shape[1]
    rows = out_t_ref.shape[2]
    queries = out_ref.shape[0]
    repeat = rows // queries
    scale = 1.0 / math.sqrt(HD)
    for head in range(HEADS):
        own_k = own_k_ref[:, head * HD : (head + 1) * HD]
        grad = nn(own_k.T, own_slope_ref[head])
        for c in range(chunks):
            grad += nn(kv_ref[(c * HEADS + head) * KINDS].T, slope_ref[head, c])
        grad = grad * scale
        out = out_t_ref[head]
        for r in range(repeat):
            cols = slice((head * repeat + r) * HD, (head * repeat + r + 1) * HD)
            at = slice(r * queries, (r + 1) * queries)
            out_ref[:, cols] = out[:, at].T.astype(jnp.bfloat16)
            grad_q_ref[:, cols] = grad[:, at].T.astype(jnp.bfloat16)


def query_rows(kv, own_k, out_t, slope, own_slope, queries, width):
    vmem = pl.BlockSpec(memory_space=pltpu.VMEM)
    shape = jax.ShapeDtypeStruct((queries, width), jnp.bfloat16)
    return pl.pallas_call(
        rows_kernel,
        out_shape=(shape, shape),
        in_specs=[vmem] * 5,
        out_specs=(vmem, vmem),
        compiler_params=pltpu.CompilerParams(vmem_limit_bytes=24 * MIB),
        cost_estimate=pl.CostEstimate(
            flops=2 * HD * HEADS * out_t.shape[2] * kv.shape[0] * kv.shape[1] // 2,
            bytes_accessed=12 * MIB,
            transcendentals=0,
        ),
        name="outputs_by_query",
    )(kv, own_k, out_t, slope, own_slope)


def zeros_kernel(out_ref):
    out_ref[...] = jnp.zeros_like(out_ref)


def zeros(rows):
    return pl.pallas_call(
        zeros_kernel,
        out_shape=jax.ShapeDtypeStruct((rows, SLICE, HD), jnp.float32),
        out_specs=pl.BlockSpec(memory_space=pltpu.VMEM),
        compiler_params=pltpu.CompilerParams(vmem_limit_bytes=16 * MIB),
        name="zero_table",
    )()


def add_kernel(index_ref, got_ref, zeros_ref, out_ref, table):
    selected = index_ref.shape[1]
    owners, held = out_ref.shape[0], out_ref.shape[1] - TAG
    blocks = held // SLICE

    def step(n, carry):
        at = [index_ref[n, k] for k in range(selected)]
        sums = [table[at[k]] + got_ref[n, k].astype(jnp.float32) for k in range(selected)]
        for k in range(selected):
            table[at[k]] = sums[k]
        return carry

    lax.fori_loop(0, got_ref.shape[0], step, 0, unroll=4)

    def finish(n, squares):
        rows = table[pl.ds(n * blocks, blocks)].reshape(held, HD)
        out_ref[n, pl.ds(0, held)] = rows.astype(jnp.bfloat16)
        return squares + jnp.sum((rows * rows).reshape(held // 8, 8, HD), axis=0)

    squares = lax.fori_loop(0, owners, finish, jnp.zeros((8, HD), jnp.float32), unroll=4)
    high = squares.astype(jnp.bfloat16).astype(jnp.float32)
    tag = jnp.concatenate([high, squares - high], axis=0).astype(jnp.bfloat16)
    for n in range(owners):
        out_ref[n, pl.ds(held, TAG)] = tag


def add_up(index, got, zeros, blk_dev):
    count = got.shape[0]
    vmem = pl.BlockSpec(memory_space=pltpu.VMEM)
    return pl.pallas_call(
        add_kernel,
        out_shape=(
            jax.ShapeDtypeStruct((count, blk_dev * SLICE + TAG, HD), jnp.bfloat16),
            jax.ShapeDtypeStruct(zeros.shape, zeros.dtype),
        ),
        in_specs=[pl.BlockSpec(memory_space=pltpu.SMEM), vmem, vmem],
        out_specs=(vmem, vmem),
        input_output_aliases={2: 1},
        compiler_params=pltpu.CompilerParams(vmem_limit_bytes=24 * MIB),
        name="add_over_readers",
    )(index, got, zeros)[0]


def finish_kernel(count, *refs):
    squares, (got_ref, key_ref, value_ref, keys, values, sems) = refs[:-6], refs[-6:]
    total = jnp.sum(sum(ref[...] for ref in squares), axis=(0, 1), keepdims=True)
    inv = 1.0 / jnp.sqrt(total / count + 1e-6)
    parts = sems.shape[0]
    step = keys.shape[0] // parts
    copies = []
    for n in range(parts):
        at = pl.ds(n * step, step)
        for m in range(got_ref.shape[0]):
            t, h, kind = m // 4, (m // 2) % 2, m % 2
            part = got_ref[m, n * step * SLICE : (n + 1) * step * SLICE].astype(jnp.float32) * inv
            part = part.reshape(step, SLICE, HD)
            (keys, values)[kind][at, t * SLICE : (t + 1) * SLICE, h * HD : (h + 1) * HD] = part
        for kind, (src, dst) in enumerate(((keys, key_ref), (values, value_ref))):
            copies.append(pltpu.make_async_copy(src.at[at], dst.at[at], sems.at[n, kind]))
            copies[-1].start()
    for copy in copies:
        copy.wait()


def finish(squares, got, block_tok, width, count):
    blocks = (got.shape[1] - TAG) // SLICE
    vmem = pl.BlockSpec(memory_space=pltpu.VMEM)
    hbm = pl.BlockSpec(memory_space=pltpu.HBM)
    shape = (blocks, block_tok, width)
    return pl.pallas_call(
        functools.partial(finish_kernel, count),
        out_shape=(jax.ShapeDtypeStruct(shape, jnp.float32),) * 2,
        in_specs=[vmem] * (len(squares) + 1),
        out_specs=(hbm, hbm),
        scratch_shapes=[
            pltpu.VMEM(shape, jnp.float32),
            pltpu.VMEM(shape, jnp.float32),
            pltpu.SemaphoreType.DMA((4, KINDS)),
        ],
        compiler_params=pltpu.CompilerParams(vmem_limit_bytes=24 * MIB),
        name="normalize_updates",
    )(*squares, got)


def swap(a):
    return lax.all_to_all(a, "wide", split_axis=0, concat_axis=0, tiled=True)


def local(
    queries,
    own_keys,
    own_values,
    cart_keys,
    cart_values,
    block_ids,
    block_home,
    query_len,
    grad_out,
):
    wide_count = lax.axis_size("wide")
    blk_dev, block_tok, width = cart_keys.shape
    selected = block_ids.shape[1]
    all_blocks = block_home.shape[0]
    held = swap(split(block_ids, block_home, cart_keys, cart_values, wide_count))
    asked = held[:, blk_dev, :2, :selected].astype(jnp.int32)
    asked, table = lax.optimization_barrier((asked, zeros(all_blocks)))
    owner, row = asked[:, 0], asked[:, 1]
    picked, used = pick(
        (owner * (blk_dev + 1) + row).reshape(-1),
        query_len,
        held.reshape(wide_count * (blk_dev + 1), SLICE, HD),
    )
    kv = swap(picked.reshape(wide_count, selected * SLICE, HD))
    send, out_t, slope, own_slope = attend(
        used, kv, queries[0], grad_out[0], own_keys[0], own_values[0]
    )
    got = swap(send).reshape(wide_count, selected, SLICE, HD)
    back = swap(add_up(owner * blk_dev + row, got, table, blk_dev))
    squares = back[:, -TAG:].astype(jnp.float32).reshape(2 * wide_count, TAG // 2, HD)
    squares = jnp.sum(squares, axis=0)
    mp = lax.axis_size("mp")
    shifts = [[(i, (i + d) % mp) for i in range(mp)] for d in range(1, mp)]
    squares = [squares] + [lax.ppermute(squares, "mp", pairs) for pairs in shifts]
    out_t, slope, _ = lax.optimization_barrier((out_t, slope, back))
    attn_out, grad_queries = query_rows(
        kv, own_keys[0], out_t, slope, own_slope, queries.shape[1], queries.shape[2]
    )
    count = 2.0 * all_blocks * block_tok * width * mp
    key_update, value_update = finish(squares, back, block_tok, width, count)
    return (attn_out[None], grad_queries[None], key_update, value_update)


def solution(mesh):
    shared = P("wide", None, "mp")
    return jax.shard_map(
        local,
        mesh=mesh,
        in_specs=(shared, shared, shared, shared, shared, P("wide", None), P(), P("wide"), shared),
        out_specs=(shared, shared, shared, shared),
        check_vma=False,
    )
```

```python
import functools
import math

import jax
import jax.numpy as jnp
from jax import lax
from jax.experimental import pallas as pl
from jax.experimental.pallas import tpu as pltpu
from jax.sharding import PartitionSpec as P

HD = 128
SLICE = 16
TAG = 8
HEADS = 2
KINDS = 2
MIB = 1024 * 1024


def nt(a, b):
    return lax.dot_general(a, b, (((1,), (1,)), ((), ())), preferred_element_type=jnp.float32)


def nn(a, b):
    return jnp.dot(a, b, preferred_element_type=jnp.float32)


def split_kernel(
    ids_ref,
    home_ref,
    keys_ref,
    values_ref,
    out_ref,
    inside,
    parts,
    ids,
    home,
    in_sems,
    out_sems,
    list_sems,
):
    blocks, tokens, width = keys_ref.shape
    groups = tokens // SLICE
    arrive = []
    for t in range(groups):
        for kind, src in enumerate((keys_ref, values_ref)):
            copy = pltpu.make_async_copy(
                src.at[:, pl.ds(t * SLICE, SLICE)], inside.at[t, kind], in_sems.at[t, kind]
            )
            copy.start()
            arrive.append(copy)
    lists = ((ids_ref, ids), (home_ref, home))
    lists = [
        pltpu.make_async_copy(src, dst, list_sems.at[n]) for n, (src, dst) in enumerate(lists)
    ]
    for copy in lists:
        copy.start()
    for copy in lists:
        copy.wait()
    line = lax.broadcasted_iota(jnp.int32, (SLICE, HD), 0)
    lane = lax.broadcasted_iota(jnp.int32, (SLICE, HD), 1)
    tag = jnp.zeros((SLICE, HD), jnp.int32)
    for k in range(ids.shape[1]):
        storage = home[ids[0, k]]
        owner = lax.div(storage, blocks)
        tag = jnp.where((line == 0) & (lane == k), owner, tag)
        tag = jnp.where((line == 1) & (lane == k), storage - owner * blocks, tag)
    tag = tag.astype(jnp.float32).astype(jnp.bfloat16)
    leave = []
    for t in range(groups):
        for kind in range(KINDS):
            arrive[t * KINDS + kind].wait()
        for part in range(HEADS * KINDS):
            m = t * HEADS * KINDS + part
            h, kind = part // KINDS, part % KINDS
            parts[m, pl.ds(0, blocks)] = inside[t, kind, :, :, h * HD : (h + 1) * HD]
            parts[m, blocks] = tag
            copy = pltpu.make_async_copy(parts.at[m], out_ref.at[m], out_sems.at[m])
            copy.start()
            leave.append(copy)
    for copy in leave:
        copy.wait()


def split(block_ids, block_home, cart_keys, cart_values, count):
    blocks, tokens, width = cart_keys.shape
    groups = tokens // SLICE
    hbm = pl.BlockSpec(memory_space=pltpu.HBM)
    return pl.pallas_call(
        split_kernel,
        out_shape=jax.ShapeDtypeStruct((count, blocks + 1, SLICE, HD), jnp.bfloat16),
        in_specs=[hbm] * 4,
        out_specs=hbm,
        scratch_shapes=[
            pltpu.VMEM((groups, KINDS, blocks, SLICE, width), jnp.bfloat16),
            pltpu.VMEM((count, blocks + 1, SLICE, HD), jnp.bfloat16),
            pltpu.SMEM(block_ids.shape, jnp.int32),
            pltpu.SMEM(block_home.shape, jnp.int32),
            pltpu.SemaphoreType.DMA((groups, KINDS)),
            pltpu.SemaphoreType.DMA((count,)),
            pltpu.SemaphoreType.DMA((2,)),
        ],
        name="split_blocks",
    )(block_ids, block_home, cart_keys, cart_values)


def pick_kernel(index_ref, length_ref, held_ref, out_ref, used_ref):
    used_ref[...] = jnp.full(used_ref.shape, length_ref[0], jnp.int32)

    def step(n, carry):
        for u in range(16):
            out_ref[n * 16 + u] = held_ref[index_ref[n * 16 + u]]
        return carry

    lax.fori_loop(0, out_ref.shape[0] // 16, step, 0, unroll=2)


def pick(index, length, held):
    smem = pl.BlockSpec(memory_space=pltpu.SMEM)
    vmem = pl.BlockSpec(memory_space=pltpu.VMEM)
    return pl.pallas_call(
        pick_kernel,
        out_shape=(
            jax.ShapeDtypeStruct((index.shape[0],) + held.shape[1:], jnp.bfloat16),
            jax.ShapeDtypeStruct((8, HD), jnp.int32),
        ),
        in_specs=[smem, smem, vmem],
        out_specs=(vmem, vmem),
        compiler_params=pltpu.CompilerParams(vmem_limit_bytes=16 * MIB),
        name="pick_requested",
    )(index, length, held)


def attend_kernel(
    length_ref,
    kv_ref,
    q_ref,
    g_ref,
    own_k_ref,
    own_v_ref,
    send_ref,
    out_ref,
    slope_ref,
    own_slope_ref,
    score,
    expo,
    acc,
    q_rows,
    g_cols,
):
    used = length_ref[0:1, 0:1]
    chunks = kv_ref.shape[0] // (HEADS * KINDS)
    chunk = kv_ref.shape[1]
    rows = q_rows.shape[0]
    queries = q_ref.shape[0]
    repeat = rows // queries
    own = own_k_ref.shape[0]
    scale = 1.0 / math.sqrt(HD)
    log2e = scale * math.log2(math.e)
    position = lax.rem(lax.broadcasted_iota(jnp.int32, (1, rows), 1), queries)
    row_used = position < used
    own_at = lax.broadcasted_iota(jnp.int32, (own, rows), 0)
    seen = (own_at <= position) & (own_at < used)
    ones = jnp.ones((16, chunk), jnp.bfloat16)
    for head in range(HEADS):
        lanes = slice(head * HD, (head + 1) * HD)
        own_k = own_k_ref[:, lanes]
        own_v = own_v_ref[:, lanes]
        at = lambda c, kind: (c * HEADS + head) * KINDS + kind
        for r in range(repeat):
            cols = slice((head * repeat + r) * HD, (head * repeat + r + 1) * HD)
            q_rows[r * queries : (r + 1) * queries] = q_ref[:, cols]
            g_cols[:, r * queries : (r + 1) * queries] = g_ref[:, cols].T
        own_s = jnp.where(seen, nt(own_k, q_rows[...]), -1e30)
        top = jnp.max(own_s.reshape(own // 8, 8, rows), axis=0)
        for c in range(chunks):
            s = nt(kv_ref[at(c, 0)], q_rows[...])
            score[c] = s
            top = jnp.maximum(top, jnp.max(s.reshape(chunk // 8, 8, rows), axis=0))
        top = jnp.max(top, axis=0, keepdims=True) * log2e
        e = jnp.exp2(own_s * log2e - top)
        own_e = e.astype(jnp.bfloat16)
        acc[...] = nn(jnp.concatenate([own_v.T, ones[:, :own]], axis=0), own_e)
        for c in range(chunks):
            e = jnp.exp2(score[c] * log2e - top)
            low = e.astype(jnp.bfloat16)
            expo[c] = low
            acc[...] += nn(jnp.concatenate([kv_ref[at(c, 1)].T, ones], axis=0), low)
        inv = 1.0 / acc[HD : HD + 1]
        g = jnp.where(row_used, g_cols[...].astype(jnp.float32), 0.0)
        out = jnp.where(row_used, acc[:HD] * inv, 0.0)
        out_ref[head] = out
        delta = jnp.sum(g * out, axis=0, keepdims=True) * inv
        gs = (g * inv).astype(jnp.bfloat16)
        ds = own_e.astype(jnp.float32) * (nn(own_v, gs) - delta)
        own_slope_ref[head] = ds.astype(jnp.bfloat16)
        for c in range(chunks):
            low = expo[c]
            send_ref[at(c, 1)] = nt(low, gs).astype(jnp.bfloat16)
            dp = nn(kv_ref[at(c, 1)], gs)
            ds = (low.astype(jnp.float32) * (dp - delta)).astype(jnp.bfloat16)
            slope_ref[head, c] = ds
            send_ref[at(c, 0)] = (nn(ds, q_rows[...]) * scale).astype(jnp.bfloat16)


def attend(length, kv, q, g, own_k, own_v):
    count, chunk, _ = kv.shape
    queries, width = q.shape
    rows = queries * width // (HEADS * HD)
    chunks = count // (HEADS * KINDS)
    vmem = pl.BlockSpec(memory_space=pltpu.VMEM)
    return pl.pallas_call(
        attend_kernel,
        out_shape=(
            jax.ShapeDtypeStruct(kv.shape, jnp.bfloat16),
            jax.ShapeDtypeStruct((HEADS, HD, rows), jnp.float32),
            jax.ShapeDtypeStruct((HEADS, chunks, chunk, rows), jnp.bfloat16),
            jax.ShapeDtypeStruct((HEADS, own_k.shape[0], rows), jnp.bfloat16),
        ),
        in_specs=[vmem] * 6,
        out_specs=(vmem,) * 4,
        scratch_shapes=[
            pltpu.VMEM((chunks, chunk, rows), jnp.float32),
            pltpu.VMEM((chunks, chunk, rows), jnp.bfloat16),
            pltpu.VMEM((HD + 16, rows), jnp.float32),
            pltpu.VMEM((rows, HD), jnp.bfloat16),
            pltpu.VMEM((HD, rows), jnp.bfloat16),
        ],
        compiler_params=pltpu.CompilerParams(vmem_limit_bytes=36 * MIB),
        cost_estimate=pl.CostEstimate(
            flops=10 * 2 * HD * rows * (chunks * chunk + queries),
            bytes_accessed=8 * MIB,
            transcendentals=HEADS * rows * chunks * chunk,
        ),
        name="attend_forward_backward",
    )(length, kv, q, g, own_k, own_v)


def rows_kernel(kv_ref, own_k_ref, out_t_ref, slope_ref, own_slope_ref, out_ref, grad_q_ref):
    chunks = slope_ref.shape[1]
    rows = out_t_ref.shape[2]
    queries = out_ref.shape[0]
    repeat = rows // queries
    scale = 1.0 / math.sqrt(HD)
    for head in range(HEADS):
        own_k = own_k_ref[:, head * HD : (head + 1) * HD]
        grad = nn(own_k.T, own_slope_ref[head])
        for c in range(chunks):
            grad += nn(kv_ref[(c * HEADS + head) * KINDS].T, slope_ref[head, c])
        grad = grad * scale
        out = out_t_ref[head]
        for r in range(repeat):
            cols = slice((head * repeat + r) * HD, (head * repeat + r + 1) * HD)
            at = slice(r * queries, (r + 1) * queries)
            out_ref[:, cols] = out[:, at].T.astype(jnp.bfloat16)
            grad_q_ref[:, cols] = grad[:, at].T.astype(jnp.bfloat16)


def query_rows(kv, own_k, out_t, slope, own_slope, queries, width):
    vmem = pl.BlockSpec(memory_space=pltpu.VMEM)
    shape = jax.ShapeDtypeStruct((queries, width), jnp.bfloat16)
    return pl.pallas_call(
        rows_kernel,
        out_shape=(shape, shape),
        in_specs=[vmem] * 5,
        out_specs=(vmem, vmem),
        compiler_params=pltpu.CompilerParams(vmem_limit_bytes=24 * MIB),
        cost_estimate=pl.CostEstimate(
            flops=2 * HD * HEADS * out_t.shape[2] * kv.shape[0] * kv.shape[1] // 2,
            bytes_accessed=12 * MIB,
            transcendentals=0,
        ),
        name="outputs_by_query",
    )(kv, own_k, out_t, slope, own_slope)


def add_kernel(index_ref, got_ref, out_ref, table):
    selected = index_ref.shape[1]
    owners, held = out_ref.shape[0], out_ref.shape[1] - TAG
    blocks = held // SLICE
    table[...] = jnp.zeros_like(table)

    def step(n, carry):
        at = [index_ref[n, k] for k in range(selected)]
        sums = [table[at[k]] + got_ref[n, k].astype(jnp.float32) for k in range(selected)]
        for k in range(selected):
            table[at[k]] = sums[k]
        return carry

    lax.fori_loop(0, got_ref.shape[0], step, 0, unroll=4)

    def finish(n, squares):
        rows = table[pl.ds(n * blocks, blocks)].reshape(held, HD)
        out_ref[n, pl.ds(0, held)] = rows.astype(jnp.bfloat16)
        return squares + jnp.sum((rows * rows).reshape(held // 8, 8, HD), axis=0)

    squares = lax.fori_loop(0, owners, finish, jnp.zeros((8, HD), jnp.float32), unroll=4)
    squares = squares[: TAG // 2] + squares[TAG // 2 :]
    high = squares.astype(jnp.bfloat16).astype(jnp.float32)
    tag = jnp.concatenate([high, squares - high], axis=0).astype(jnp.bfloat16)
    for n in range(owners):
        out_ref[n, pl.ds(held, TAG)] = tag


def add_up(index, got, blk_dev):
    count = got.shape[0]
    vmem = pl.BlockSpec(memory_space=pltpu.VMEM)
    return pl.pallas_call(
        add_kernel,
        out_shape=jax.ShapeDtypeStruct((count, blk_dev * SLICE + TAG, HD), jnp.bfloat16),
        in_specs=[pl.BlockSpec(memory_space=pltpu.SMEM), vmem],
        out_specs=vmem,
        scratch_shapes=[pltpu.VMEM((count * blk_dev, SLICE, HD), jnp.float32)],
        compiler_params=pltpu.CompilerParams(vmem_limit_bytes=24 * MIB),
        name="add_over_readers",
    )(index, got)


def finish_kernel(count, *refs):
    squares, (got_ref, key_ref, value_ref, keys, values, sems) = refs[:-6], refs[-6:]
    total = jnp.sum(sum(ref[...] for ref in squares), axis=(0, 1), keepdims=True)
    inv = 1.0 / jnp.sqrt(total / count + 1e-6)
    parts = sems.shape[0]
    step = keys.shape[0] // parts
    copies = []
    for n in range(parts):
        at = pl.ds(n * step, step)
        for m in range(got_ref.shape[0]):
            t, h, kind = m // 4, (m // 2) % 2, m % 2
            part = got_ref[m, n * step * SLICE : (n + 1) * step * SLICE].astype(jnp.float32) * inv
            part = part.reshape(step, SLICE, HD)
            (keys, values)[kind][at, t * SLICE : (t + 1) * SLICE, h * HD : (h + 1) * HD] = part
        for kind, (src, dst) in enumerate(((keys, key_ref), (values, value_ref))):
            copies.append(pltpu.make_async_copy(src.at[at], dst.at[at], sems.at[n, kind]))
            copies[-1].start()
    for copy in copies:
        copy.wait()


def finish(squares, got, block_tok, width, count):
    blocks = (got.shape[1] - TAG) // SLICE
    vmem = pl.BlockSpec(memory_space=pltpu.VMEM)
    hbm = pl.BlockSpec(memory_space=pltpu.HBM)
    shape = (blocks, block_tok, width)
    return pl.pallas_call(
        functools.partial(finish_kernel, count),
        out_shape=(jax.ShapeDtypeStruct(shape, jnp.float32),) * 2,
        in_specs=[vmem] * (len(squares) + 1),
        out_specs=(hbm, hbm),
        scratch_shapes=[
            pltpu.VMEM(shape, jnp.float32),
            pltpu.VMEM(shape, jnp.float32),
            pltpu.SemaphoreType.DMA((4, KINDS)),
        ],
        compiler_params=pltpu.CompilerParams(vmem_limit_bytes=24 * MIB),
        name="normalize_updates",
    )(*squares, got)


def swap(a):
    return lax.all_to_all(a, "wide", split_axis=0, concat_axis=0, tiled=True)


def local(
    queries,
    own_keys,
    own_values,
    cart_keys,
    cart_values,
    block_ids,
    block_home,
    query_len,
    grad_out,
):
    wide_count = lax.axis_size("wide")
    blk_dev, block_tok, width = cart_keys.shape
    selected = block_ids.shape[1]
    all_blocks = block_home.shape[0]
    held = swap(split(block_ids, block_home, cart_keys, cart_values, wide_count))
    asked = held[:, blk_dev, :2, :selected].astype(jnp.int32)
    owner, row = asked[:, 0], asked[:, 1]
    picked, used = pick(
        (owner * (blk_dev + 1) + row).reshape(-1),
        query_len,
        held.reshape(wide_count * (blk_dev + 1), SLICE, HD),
    )
    kv = swap(picked.reshape(wide_count, selected * SLICE, HD))
    send, out_t, slope, own_slope = attend(
        used, kv, queries[0], grad_out[0], own_keys[0], own_values[0]
    )
    got = swap(send).reshape(wide_count, selected, SLICE, HD)
    back = swap(add_up(owner * blk_dev + row, got, blk_dev))
    squares = jnp.sum(back[:, -TAG:].astype(jnp.float32), axis=0)
    mp = lax.axis_size("mp")
    shifts = [[(i, (i + d) % mp) for i in range(mp)] for d in range(1, mp)]
    squares = [squares] + [lax.ppermute(squares, "mp", pairs) for pairs in shifts]
    out_t, slope, _ = lax.optimization_barrier((out_t, slope, back))
    attn_out, grad_queries = query_rows(
        kv, own_keys[0], out_t, slope, own_slope, queries.shape[1], queries.shape[2]
    )
    count = 2.0 * all_blocks * block_tok * width * mp
    key_update, value_update = finish(squares, back, block_tok, width, count)
    return (attn_out[None], grad_queries[None], key_update, value_update)


def solution(mesh):
    shared = P("wide", None, "mp")
    return jax.shard_map(
        local,
        mesh=mesh,
        in_specs=(shared, shared, shared, shared, shared, P("wide", None), P(), P("wide"), shared),
        out_specs=(shared, shared, shared, shared),
        check_vma=False,
    )
```
